128 devices in a mesh: bin: 8 (over x, core), freq: 16 (over z, y).
Axes of the slice: x: 4, y: 4, z: 4, core: 2. Of those that a mesh axis runs over, the one named last changes fastest.
Arguments:
- traces: bfloat16 [131072, 2048], P(('bin', 'freq')), may hold values from -6 to 6
- rcv_index: int32 [131072], P(('bin', 'freq')), may hold values from 0 to 511, as said below
- src_index: int32 [131072], P(('bin', 'freq')), may hold values from 0 to 511, as said below
- wave_filter: float32 [2, 256], P(None, 'freq'), may hold values from -8 to 8
Outputs:
- multiples: bfloat16 [2, 256, 512, 512], P(None, 'freq', 'bin')
The draws below stay inside these ranges and needn't reach their ends.
Inputs may be any that keep to these rules, and one draw needn't show every extreme that they name: rcv_index and src_index name each (receiver, source) cell at most once. Group the receiver bins in runs of 4 consecutive ones: every device holds the same number of traces of a given run, at most 16, and in some run exactly 16 on every device. `src_index`: source bin of the trace, paired with rcv_index as above.
All inputs are finite; a program needn't handle non-finite values.
Results may differ from the reference program's by a relative error of at most 0.0058.
Values may be sent and summed in bfloat16 or wider, within the bound.
A program may use at most 128 MiB of HBM per device.

```python
import math
import jax
import jax.numpy as jnp
from jax import lax

ORDER = 512
NT = 2048
NF = 256
TRACES = 131072
TR_DEV = 1024
ROWS_OWN = 4
N_BIN = 8
N_FREQ = 16


def covered_cells(key):
    owners = N_BIN * N_FREQ
    quarter = TR_DEV // (2 * owners)
    key_weight, key_send, key_owner = jax.random.split(key, 3)
    shuffled = jax.random.permutation(key_weight, owners)
    resident_block = jnp.zeros((owners,), jnp.int32).at[shuffled].set(jnp.arange(owners, dtype=jnp.int32))
    weight = jnp.where(resident_block < owners // 4, 4, jnp.where(resident_block < owners // 2, 2, 1)).astype(jnp.int32)
    piece_size = weight * quarter
    starts = (jnp.cumsum(piece_size) - piece_size).astype(jnp.int32)
    send_keys = jax.random.split(key_send, owners)
    arrival = jax.vmap(lambda single: jax.random.permutation(single, TR_DEV))(send_keys).astype(jnp.int32)
    target = jnp.sum((arrival[:, :, None] >= starts[None, None, 1:]).astype(jnp.int32), axis=2)
    offset = arrival - starts[target]
    sender = jnp.arange(owners, dtype=jnp.int32)[:, None]
    position = sender * piece_size[target] + offset
    owner_keys = jax.random.split(key_owner, owners)
    placement = jax.vmap(lambda single: jax.random.permutation(single, 2 * TR_DEV))(owner_keys).astype(jnp.int32)
    cell_index = placement[target, position]
    receiver = target * ROWS_OWN + cell_index // ORDER
    source = cell_index % ORDER
    return (receiver.reshape(-1).astype(jnp.int32), source.reshape(-1).astype(jnp.int32))


def draw_rcv_index(key, part):
    receiver, source = covered_cells(key)
    return receiver


def draw_src_index(key, part):
    receiver, source = covered_cells(key)
    return source


def steps_of(key, extent, cuts, smallest, top_value):
    loudness = 1.0
    for dim, parts in cuts:
        draws = jax.random.uniform(jax.random.fold_in(jax.random.fold_in(key, 6), dim), (parts,), jnp.float32, smallest / len(cuts), top_value / len(cuts))
        loudness = loudness * jnp.repeat(jnp.exp(draws), extent[dim] // parts).reshape((-1,) + (1,) * (len(extent) - 1 - dim))
    return loudness


def normal_values(stream_key, dims, width, limit, cuts=(), kind=jnp.bfloat16):
    gain = steps_of(stream_key, dims, cuts, -0.22, 0.18) if cuts else 1.0
    drawn = jax.random.normal(stream_key, dims, jnp.float32) * width * gain
    return jnp.minimum(jnp.maximum(drawn, -limit), limit).astype(kind)


def setup_inputs(seed: int = 0) -> dict:
    splits = jax.random.split(jax.random.key(seed), 5)
    traces = normal_values(splits[0], (TRACES, NT), 1.0, 6.0, ((0, 128),))
    rcv_index = draw_rcv_index(jax.random.fold_in(splits[4], 71), 0)
    src_index = draw_src_index(jax.random.fold_in(splits[4], 71), 0)
    wave_filter = normal_values(splits[3], (2, NF), 2.0, 8.0, ((1, 16),), jnp.float32)
    return dict(traces=traces, rcv_index=rcv_index, src_index=src_index, wave_filter=wave_filter)


def block_spectrum(block):
    values = jnp.fft.rfft(block.astype(jnp.float32), axis=1)[:, :NF] / math.sqrt(NT)
    return (jnp.real(values).astype(jnp.bfloat16), jnp.imag(values).astype(jnp.bfloat16))

def reference(traces, rcv_index, src_index, wave_filter):
    blocks = traces.reshape(16, -1, NT)
    spec_real, spec_imag = lax.map(block_spectrum, blocks)
    spec_real = spec_real.reshape(-1, NF)
    spec_imag = spec_imag.reshape(-1, NF)
    cell_index = (rcv_index * ORDER + src_index).astype(jnp.int32)
    data_real = jnp.zeros((ORDER * ORDER, NF), jnp.bfloat16).at[cell_index].set(spec_real)
    trace_imaginary = jnp.zeros((ORDER * ORDER, NF), jnp.bfloat16).at[cell_index].set(spec_imag)
    data_real = data_real.T.reshape(NF, ORDER, ORDER)
    trace_imaginary = trace_imaginary.T.reshape(NF, ORDER, ORDER)
    amplitude = 1.0 / math.sqrt(ORDER)

    def one_frequency(inputs):
        part_real, part_imag, filter_real, filter_imag = inputs
        left_real = part_real.astype(jnp.float32)
        left_imag = part_imag.astype(jnp.float32)
        highest = lax.Precision.HIGHEST
        prod_real = jnp.dot(left_real, left_real, precision=highest) - jnp.dot(left_imag, left_imag, precision=highest)
        prod_imag = jnp.dot(left_real, left_imag, precision=highest) + jnp.dot(left_imag, left_real, precision=highest)
        out_real = (filter_real * prod_real - filter_imag * prod_imag) * amplitude
        out_imag = (filter_real * prod_imag + filter_imag * prod_real) * amplitude
        return (out_real.astype(jnp.bfloat16), out_imag.astype(jnp.bfloat16))
    out_real, out_imag = lax.map(one_frequency, (data_real, trace_imaginary, wave_filter[0], wave_filter[1]))
    return jnp.stack([out_real, out_imag])
```

```python
import functools
import math

import jax
import jax.numpy as jnp
import numpy as np
from jax import lax
from jax.experimental import pallas as pl
from jax.experimental.pallas import tpu as pltpu
from jax.sharding import PartitionSpec as P
import ml_dtypes

ORDER = 512
NT = 2048
NF = 256
DEV = 128
TR = 1024
F32 = jnp.float32
BF16 = jnp.bfloat16
I32 = jnp.int32
LIMIT = 56 * 1024 * 1024


def dft_tables():
    comp = np.arange(4)[:, None]
    dev = np.arange(DEV)[None, :]
    freq = ((dev % 16) * 16 + (dev // 16) * 2 + comp // 2).reshape(-1)
    part = np.broadcast_to(comp % 2, (4, DEV)).reshape(-1)
    phase = (np.arange(NT)[:, None] * freq[None, :]) % NT
    angle = 2.0 * np.pi / NT * phase
    table = np.where(part[None, :] == 0, np.cos(angle), -np.sin(angle)) / math.sqrt(NT)
    high = table.astype(ml_dtypes.bfloat16)
    low = (table - high.astype(np.float64)).astype(ml_dtypes.bfloat16)
    return high, low


def index_kernel(rcv_ref, src_ref, order_ref, slots_ref, count_ref, start_ref):
    rcv = rcv_ref[...]
    src = src_ref[...]
    lane = lax.broadcasted_iota(I32, (TR, DEV), 1)
    member = (rcv // 4 == lane).astype(F32)
    row_i = lax.broadcasted_iota(I32, (DEV, DEV), 0)
    col_i = lax.broadcasted_iota(I32, (DEV, DEV), 1)
    lower = (col_i < row_i).astype(BF16)
    upper = (row_i < col_i).astype(BF16)
    carry = jnp.zeros((1, DEV), F32)
    ranks = []
    for blk in range(TR // DEV):
        m = member[blk * DEV : (blk + 1) * DEV]
        ranks.append(jnp.dot(lower, m.astype(BF16), preferred_element_type=F32) + carry)
        carry = carry + jnp.sum(m, axis=0, keepdims=True)
    rank_all = jnp.concatenate(ranks, axis=0)
    counts8 = jnp.broadcast_to(carry, (8, DEV))
    start = jnp.dot(counts8.astype(BF16), upper, preferred_element_type=F32)
    rank = jnp.sum(member * rank_all, axis=1, keepdims=True)
    first = jnp.sum(member * start[0:1], axis=1, keepdims=True)
    order_ref[...] = (rank + first).astype(I32)
    count_ref[...] = counts8.astype(I32)
    start_ref[...] = start.astype(I32)
    high = ((src // 128) * 4 + rcv % 4 + 1).astype(F32)
    low = (src % 128).astype(F32)
    value = jnp.where(lane < 16, high, jnp.where(lane < 32, low, 0.0))
    value = jnp.where(rank.astype(I32) == lane % 16, value, 0.0)
    slots_ref[...] = lax.dot_general(
        member.astype(BF16), value.astype(BF16), (((0,), (0,)), ((), ())), preferred_element_type=F32
    ).astype(BF16)


def inverse_kernel(slots_ref, code_ref):
    slots = slots_ref[...].astype(F32).T
    sub16 = lax.broadcasted_iota(I32, (16, DEV), 0).astype(F32)
    sub128 = lax.broadcasted_iota(I32, (DEV, DEV), 0).astype(F32)
    dev = lax.broadcasted_iota(I32, (16, DEV), 1).astype(F32)
    acc = jnp.zeros((32, DEV), F32)
    for j in range(16):
        hit = slots[j : j + 1] == sub16 + 1.0
        left = jnp.concatenate([jnp.where(hit, float(j + 1), 0.0), jnp.where(hit, dev, 0.0)], axis=0)
        right = (slots[16 + j : 17 + j] == sub128).astype(F32)
        acc = acc + lax.dot_general(
            left.astype(BF16), right.astype(BF16), (((1,), (1,)), ((), ())), preferred_element_type=F32
        )
    slot = acc[:16]
    code = jnp.where(slot > 0.5, (slot - 1.0) * 128.0 + acc[16:], 4096.0)
    code_ref[...] = code.astype(I32).astype(jnp.int16)


def spectrum_kernel(steps, traces_ref, high_ref, low_ref, order_ref, out_ref, acc_ref):
    step = pl.program_id(0)

    @pl.when(step == 0)
    def _():
        acc_ref[...] = jnp.zeros_like(acc_ref)

    x = traces_ref[...]
    acc_ref[...] += jnp.dot(x, high_ref[...], preferred_element_type=F32) + jnp.dot(
        x, low_ref[...], preferred_element_type=F32
    )

    @pl.when(step == steps - 1)
    def _():
        pick = (order_ref[...] == lax.broadcasted_iota(I32, (TR, TR), 1)).astype(F32).astype(BF16)
        for comp in range(4):
            spec = acc_ref[:, comp * DEV : (comp + 1) * DEV].astype(BF16)
            out_ref[:, comp * TR : (comp + 1) * TR] = lax.dot_general(
                spec, pick, (((0,), (0,)), ((), ())), preferred_element_type=F32
            ).astype(BF16)


def product_kernel(filt_ref, count_ref, start_ref, data_ref, code_ref, out_ref, rows_ref, dense_ref):
    for comp in range(4):
        for blk in range(8):
            base = comp * TR + blk * DEV
            rows_ref[pl.ds(base, DEV), :] = data_ref[:, base : base + DEV].astype(F32).T
    rows_ref[pl.ds(4 * TR, 8), :] = jnp.zeros((8, DEV), F32)

    def run_cells(run):
        count = count_ref[0, run]
        start = start_ref[0, run]
        code = code_ref[run].astype(I32)
        cols = [(code & 127)[8 * v : 8 * v + 8] for v in range(2)]
        slot = [(code >> 7)[8 * v : 8 * v + 8] for v in range(2)]

        def one_slot(step, acc):
            acc = list(acc)
            for u in range(4):
                j = step * 4 + u
                hit = [slot[v] == j for v in range(2)]
                for comp in range(4):
                    row = jnp.broadcast_to(rows_ref[pl.ds(comp * TR + start + j, 1), :], (8, DEV))
                    for v in range(2):
                        got = jnp.take_along_axis(row, cols[v], axis=1, mode="promise_in_bounds")
                        acc[2 * comp + v] = jnp.where(hit[v], got, acc[2 * comp + v])
            return tuple(acc)

        return lax.fori_loop(0, (count + 3) // 4, one_slot, (jnp.zeros((8, DEV), F32),) * 8)

    top = lax.broadcasted_iota(I32, (8, DEV), 0) < 4

    def two_runs(pair, _):
        even = run_cells(2 * pair)
        odd = run_cells(2 * pair + 1)
        for comp in range(4):
            at = pl.ds(pl.multiple_of(comp * ORDER + pair * 8, 8), 8)
            for v in range(2):
                a, b = even[2 * comp + v], odd[2 * comp + v]
                dense_ref[at, pl.ds(2 * v * DEV, DEV)] = jnp.where(top, a, pltpu.roll(b, 4, 0))
                dense_ref[at, pl.ds((2 * v + 1) * DEV, DEV)] = jnp.where(top, pltpu.roll(a, 4, 0), b)
        return 0

    lax.fori_loop(0, DEV // 2, two_runs, 0)

    mine = lax.axis_index("bin") * 2
    amplitude = 1.0 / math.sqrt(ORDER)
    for i in range(2):
        real = dense_ref[pl.ds(2 * i * ORDER, ORDER), :].astype(BF16)
        imag = dense_ref[pl.ds((2 * i + 1) * ORDER, ORDER), :].astype(BF16)
        fr = filt_ref[0, mine + i]
        fi = filt_ref[1, mine + i]
        for t in range(2):
            cols = slice(t * 256, (t + 1) * 256)
            rc, ic = real[:, cols], imag[:, cols]
            dot = functools.partial(jnp.dot, preferred_element_type=F32)
            sr = dot(real, rc) - dot(imag, ic)
            si = dot(real, ic) + dot(imag, rc)
            outr = ((fr * sr - fi * si) * amplitude).astype(BF16)
            outi = ((fr * si + fi * sr) * amplitude).astype(BF16)
            for b in range(8):
                out_ref[b, 0, i, :, cols] = outr[b * 64 : (b + 1) * 64]
                out_ref[b, 1, i, :, cols] = outi[b * 64 : (b + 1) * 64]


def local(traces, rcv_index, src_index, wave_filter):
    high, low = dft_tables()
    params = pltpu.CompilerParams(vmem_limit_bytes=LIMIT)
    vmem = pl.BlockSpec(memory_space=pltpu.VMEM)
    smem = pl.BlockSpec(memory_space=pltpu.SMEM)
    shape = jax.ShapeDtypeStruct
    order, slots, count, start = pl.pallas_call(
        index_kernel,
        out_shape=(shape((TR, 1), I32), shape((DEV, DEV), BF16), shape((8, DEV), I32), shape((8, DEV), I32)),
        compiler_params=params,
        name="index",
    )(rcv_index.reshape(TR, 1), src_index.reshape(TR, 1))
    slots = lax.all_to_all(slots, ("bin", "freq"), split_axis=0, concat_axis=0, tiled=True)
    steps = 4
    depth = NT // steps
    spectra = pl.pallas_call(
        functools.partial(spectrum_kernel, steps),
        grid=(steps,),
        in_specs=[
            pl.BlockSpec((TR, depth), lambda k: (0, k)),
            pl.BlockSpec((depth, 4 * DEV), lambda k: (k, 0)),
            pl.BlockSpec((depth, 4 * DEV), lambda k: (k, 0)),
            pl.BlockSpec((TR, 1), lambda k: (0, 0)),
        ],
        out_specs=pl.BlockSpec((DEV, 4 * TR), lambda k: (0, 0)),
        out_shape=shape((DEV, 4 * TR), BF16),
        scratch_shapes=[pltpu.VMEM((TR, 4 * DEV), F32)],
        compiler_params=params,
        cost_estimate=pl.CostEstimate(flops=5 * 10**9, bytes_accessed=9 * 10**6, transcendentals=0),
        name="spectrum",
    )(traces, jnp.asarray(high), jnp.asarray(low), order)
    spectra = lax.all_to_all(spectra, ("bin", "freq"), split_axis=0, concat_axis=0, tiled=True)
    code = pl.pallas_call(
        inverse_kernel, out_shape=shape((16, DEV), jnp.int16), compiler_params=params, name="inverse"
    )(slots)
    code = lax.all_gather(code, ("bin", "freq"), axis=0)
    rows = pl.pallas_call(
        product_kernel,
        in_specs=[smem, smem, smem, vmem, vmem],
        out_specs=vmem,
        out_shape=shape((8, 2, 2, 64, ORDER), BF16),
        scratch_shapes=[pltpu.VMEM((4 * TR + 8, DEV), F32), pltpu.VMEM((4 * ORDER, ORDER), F32)],
        compiler_params=params,
        name="product",
    )(wave_filter, count, start, spectra, code)
    rows = lax.all_to_all(rows, "bin", split_axis=0, concat_axis=0, tiled=True)
    return rows.transpose(1, 0, 2, 3, 4).reshape(2, 16, 64, ORDER)


def solution(mesh):
    placed = (P(("bin", "freq"), None), P(("bin", "freq")), P(("bin", "freq")), P(None, "freq"))
    return jax.shard_map(
        local, mesh=mesh, in_specs=placed, out_specs=P(None, "freq", "bin", None), check_vma=False
    )
```

```python
import functools
import math

import jax
import jax.numpy as jnp
import numpy as np
from jax import lax
from jax.experimental import pallas as pl
from jax.experimental.pallas import tpu as pltpu
from jax.sharding import PartitionSpec as P
import ml_dtypes

ORDER = 512
NT = 2048
NF = 256
DEV = 128
TR = 1024
F32 = jnp.float32
BF16 = jnp.bfloat16
I32 = jnp.int32
LIMIT = 56 * 1024 * 1024


def dft_tables():
    comp = np.arange(4)[:, None]
    dev = np.arange(DEV)[None, :]
    freq = ((dev % 16) * 16 + (dev // 16) * 2 + comp // 2).reshape(-1)
    part = np.broadcast_to(comp % 2, (4, DEV)).reshape(-1)
    phase = (np.arange(NT)[:, None] * freq[None, :]) % NT
    angle = 2.0 * np.pi / NT * phase
    table = np.where(part[None, :] == 0, np.cos(angle), -np.sin(angle)) / math.sqrt(NT)
    high = table.astype(ml_dtypes.bfloat16)
    low = (table - high.astype(np.float64)).astype(ml_dtypes.bfloat16)
    return high, low


def index_kernel(rcv_ref, src_ref, order_ref, cell_ref, count_ref, start_ref, list_ref, edge_ref):
    lane = lax.broadcasted_iota(I32, (TR, DEV), 1)
    row_i = lax.broadcasted_iota(I32, (DEV, DEV), 0)
    col_i = lax.broadcasted_iota(I32, (DEV, DEV), 1)
    lower = (col_i < row_i).astype(BF16)
    upper = (row_i < col_i).astype(BF16)
    same = row_i == col_i
    rcv_cols, src_cols = [], []
    for blk in range(TR // DEV):
        for cols, ref in ((rcv_cols, rcv_ref), (src_cols, src_ref)):
            spread = jnp.where(same, jnp.broadcast_to(ref[blk : blk + 1, :], (DEV, DEV)), 0)
            cols.append(jnp.sum(spread.astype(F32), axis=1, keepdims=True).astype(I32))
    rcv = jnp.concatenate(rcv_cols, axis=0)
    src = jnp.concatenate(src_cols, axis=0)
    member = (rcv // 4 == lane).astype(F32)
    carry = jnp.zeros((1, DEV), F32)
    ranks = []
    for blk in range(TR // DEV):
        m = member[blk * DEV : (blk + 1) * DEV]
        ranks.append(jnp.dot(lower, m.astype(BF16), preferred_element_type=F32) + carry)
        carry = carry + jnp.sum(m, axis=0, keepdims=True)
    rank_all = jnp.concatenate(ranks, axis=0)
    counts8 = jnp.broadcast_to(carry, (8, DEV))
    start = jnp.dot(counts8.astype(BF16), upper, preferred_element_type=F32)
    place = jnp.sum(member * (rank_all + start[0:1]), axis=1, keepdims=True).astype(I32)
    order_ref[...] = place
    count_ref[...] = counts8.astype(I32)
    start_ref[...] = start.astype(I32)
    high = ((src // 128) * 4 + rcv % 4).astype(F32)
    low = (src % 128).astype(F32)
    digit = lax.broadcasted_iota(I32, (TR, DEV), 1)
    digits = jnp.where(digit == 0, high, jnp.where(digit == 1, low, 0.0)).astype(BF16)
    pick = (place == lax.broadcasted_iota(I32, (TR, TR), 1)).astype(F32).astype(BF16)
    both = lax.dot_general(digits, pick, (((0,), (0,)), ((), ())), preferred_element_type=F32)
    cell_ref[...] = (both[0:1] * 128.0 + both[1:2]).astype(I32)
    cls = [carry <= 4.0, (carry > 4.0) & (carry <= 8.0), carry > 8.0]
    base = jnp.zeros((1, 1), F32)
    spot = jnp.zeros((1, DEV), F32)
    edges = []
    for kind in cls:
        ind = kind.astype(F32)
        before = jnp.dot(jnp.broadcast_to(ind, (8, DEV)).astype(BF16), upper, preferred_element_type=F32)[0:1]
        spot = spot + ind * (before + base)
        base = base + jnp.sum(ind, axis=1, keepdims=True)
        edges.append(base)
    here = (jnp.broadcast_to(spot, (DEV, DEV)) == row_i.astype(F32)).astype(BF16)
    names = lax.broadcasted_iota(I32, (8, DEV), 1).astype(F32).astype(BF16)
    list_ref[...] = lax.dot_general(
        names, here, (((1,), (1,)), ((), ())), preferred_element_type=F32
    ).astype(I32)
    edge_lane = lax.broadcasted_iota(I32, (8, DEV), 1)
    edge = jnp.where(edge_lane == 0, edges[0], jnp.where(edge_lane == 1, edges[1], edges[2]))
    edge_ref[...] = edge.astype(I32)


def spectrum_kernel(steps, traces_ref, high_ref, low_ref, order_ref, out_ref, acc_ref):
    step = pl.program_id(0)

    @pl.when(step == 0)
    def _():
        acc_ref[...] = jnp.zeros_like(acc_ref)

    x = traces_ref[...]
    acc_ref[...] += jnp.dot(x, high_ref[...], preferred_element_type=F32) + jnp.dot(
        x, low_ref[...], preferred_element_type=F32
    )

    @pl.when(step == steps - 1)
    def _():
        pick = (order_ref[...] == lax.broadcasted_iota(I32, (TR, TR), 1)).astype(F32).astype(BF16)
        for comp in range(4):
            spec = acc_ref[:, comp * DEV : (comp + 1) * DEV].astype(BF16)
            out_ref[:, comp * TR : (comp + 1) * TR] = lax.dot_general(
                spec, pick, (((0,), (0,)), ((), ())), preferred_element_type=F32
            ).astype(BF16)


def product_kernel(
    filt_ref, count_ref, start_ref, list_ref, edge_ref, data_ref, code_ref, out_ref, rows_ref, cell_ref, raw_ref, dense_ref
):
    stride = TR + 16
    for blk in range(8):
        cols = slice(blk * DEV, (blk + 1) * DEV)
        for comp in range(4):
            base = comp * TR + blk * DEV
            rows_ref[pl.ds(comp * stride + blk * DEV, DEV), :] = data_ref[:, base : base + DEV].astype(F32).T
        code = code_ref[:, cols].T
        cell_ref[pl.ds(blk * DEV, DEV), :] = (code // 128).astype(F32)
        cell_ref[pl.ds(stride + blk * DEV, DEV), :] = (code % 128).astype(F32)
    pad = jnp.zeros((16, DEV), F32)
    for comp in range(4):
        rows_ref[pl.ds(comp * stride + TR, 16), :] = pad
    for digit in range(2):
        cell_ref[pl.ds(digit * stride + TR, 16), :] = pad

    sub16 = lax.broadcasted_iota(I32, (16, DEV), 0).astype(F32)
    sub128 = lax.broadcasted_iota(I32, (DEV, DEV), 0).astype(F32).astype(BF16)
    one, zero = jnp.ones((), BF16), jnp.zeros((), BF16)

    def lay_out(run, size):
        count = count_ref[0, run]
        start = start_ref[0, run]
        left, right = [], []
        for j in range(size):
            at = start + j
            high = jnp.broadcast_to(cell_ref[pl.ds(at, 1), :], (16, DEV))
            hit = jnp.where(j < count, high, -1.0) == sub16
            parts = []
            for comp in range(4):
                row = jnp.broadcast_to(rows_ref[pl.ds(comp * stride + at, 1), :], (16, DEV))
                parts.append(jnp.where(hit, row, 0.0).astype(BF16))
            left.append(jnp.concatenate(parts, axis=0))
            low = jnp.broadcast_to(cell_ref[pl.ds(stride + at, 1), :], (16, DEV)).astype(BF16)
            right.append(jnp.where(jnp.concatenate([low] * 8, axis=0) == sub128, one, zero))
        raw_ref[run] = lax.dot_general(
            jnp.concatenate(left, axis=1),
            jnp.concatenate(right, axis=1),
            (((1,), (1,)), ((), ())),
            preferred_element_type=F32,
        )

    begin = 0
    for kind, (size, together) in enumerate(((4, 4), (8, 4), (16, 2))):
        end = edge_ref[0, kind]

        def some_runs(step, _, begin=begin, end=end, size=size, together=together):
            for u in range(together):
                lay_out(list_ref[0, jnp.minimum(begin + step * together + u, end - 1)], size)
            return 0

        lax.fori_loop(0, (end - begin + together - 1) // together, some_runs, 0)
        begin = end

    top = lax.broadcasted_iota(I32, (8, DEV), 0) < 4

    def four_runs(group, _):
        for comp in range(4):
            at = pl.ds(pl.multiple_of(comp * ORDER + group * 16, 16), 16)
            for v in range(2):
                sl = pl.ds(comp * 16 + 8 * v, 8)
                a, b, c, d = [raw_ref[4 * group + u, sl, :] for u in range(4)]
                first = [jnp.where(top, a, pltpu.roll(b, 4, 0)), jnp.where(top, c, pltpu.roll(d, 4, 0))]
                last = [jnp.where(top, pltpu.roll(a, 4, 0), b), jnp.where(top, pltpu.roll(c, 4, 0), d)]
                dense_ref[at, pl.ds(2 * v * DEV, DEV)] = jnp.concatenate(first, axis=0).astype(BF16)
                dense_ref[at, pl.ds((2 * v + 1) * DEV, DEV)] = jnp.concatenate(last, axis=0).astype(BF16)
        return 0

    lax.fori_loop(0, DEV // 4, four_runs, 0, unroll=2)

    mine = lax.axis_index("bin") * 2
    amplitude = 1.0 / math.sqrt(ORDER)
    for i in range(2):
        real = dense_ref[pl.ds(2 * i * ORDER, ORDER), :]
        imag = dense_ref[pl.ds((2 * i + 1) * ORDER, ORDER), :]
        fr = filt_ref[0, mine + i]
        fi = filt_ref[1, mine + i]
        for t in range(2):
            cols = slice(t * 256, (t + 1) * 256)
            rc, ic = real[:, cols], imag[:, cols]
            dot = functools.partial(jnp.dot, preferred_element_type=F32)
            sr = dot(real, rc) - dot(imag, ic)
            si = dot(real, ic) + dot(imag, rc)
            outr = ((fr * sr - fi * si) * amplitude).astype(BF16)
            outi = ((fr * si + fi * sr) * amplitude).astype(BF16)
            for b in range(8):
                out_ref[b, 0, i, :, cols] = outr[b * 64 : (b + 1) * 64]
                out_ref[b, 1, i, :, cols] = outi[b * 64 : (b + 1) * 64]


def local(traces, rcv_index, src_index, wave_filter):
    high, low = dft_tables()
    params = pltpu.CompilerParams(vmem_limit_bytes=LIMIT)
    vmem = pl.BlockSpec(memory_space=pltpu.VMEM)
    smem = pl.BlockSpec(memory_space=pltpu.SMEM)
    shape = jax.ShapeDtypeStruct
    small = shape((8, DEV), I32)
    order, cells, count, start, listed, edge = pl.pallas_call(
        index_kernel,
        out_shape=(shape((TR, 1), I32), shape((1, TR), I32), small, small, small, small),
        compiler_params=params,
        name="index",
    )(rcv_index.reshape(8, DEV), src_index.reshape(8, DEV))
    cells = lax.all_gather(cells, ("bin", "freq"), axis=0, tiled=True)
    steps = 4
    depth = NT // steps
    spectra = pl.pallas_call(
        functools.partial(spectrum_kernel, steps),
        grid=(steps,),
        in_specs=[
            pl.BlockSpec((TR, depth), lambda k: (0, k)),
            pl.BlockSpec((depth, 4 * DEV), lambda k: (k, 0)),
            pl.BlockSpec((depth, 4 * DEV), lambda k: (k, 0)),
            pl.BlockSpec((TR, 1), lambda k: (0, 0)),
        ],
        out_specs=pl.BlockSpec((DEV, 4 * TR), lambda k: (0, 0)),
        out_shape=shape((DEV, 4 * TR), BF16),
        scratch_shapes=[pltpu.VMEM((TR, 4 * DEV), F32)],
        compiler_params=params,
        cost_estimate=pl.CostEstimate(flops=5 * 10**9, bytes_accessed=9 * 10**6, transcendentals=0),
        name="spectrum",
    )(traces, jnp.asarray(high), jnp.asarray(low), order)
    spectra = lax.all_to_all(spectra, ("bin", "freq"), split_axis=0, concat_axis=0, tiled=True)
    rows = pl.pallas_call(
        product_kernel,
        in_specs=[smem, smem, smem, smem, smem, vmem, vmem],
        out_specs=vmem,
        out_shape=shape((8, 2, 2, 64, ORDER), BF16),
        scratch_shapes=[
            pltpu.VMEM((4 * (TR + 16), DEV), F32),
            pltpu.VMEM((2 * (TR + 16), DEV), F32),
            pltpu.VMEM((DEV, 64, DEV), F32),
            pltpu.VMEM((4 * ORDER, ORDER), BF16),
        ],
        compiler_params=params,
        name="product",
    )(wave_filter, count, start, listed, edge, spectra, cells)
    rows = lax.all_to_all(rows, "bin", split_axis=0, concat_axis=0, tiled=True)
    return rows.transpose(1, 0, 2, 3, 4).reshape(2, 16, 64, ORDER)


def solution(mesh):
    placed = (P(("bin", "freq"), None), P(("bin", "freq")), P(("bin", "freq")), P(None, "freq"))
    return jax.shard_map(
        local, mesh=mesh, in_specs=placed, out_specs=P(None, "freq", "bin", None), check_vma=False
    )
```

```python
import functools
import math

import jax
import jax.numpy as jnp
import numpy as np
from jax import lax
from jax.experimental import pallas as pl
from jax.experimental.pallas import tpu as pltpu
from jax.sharding import PartitionSpec as P
import ml_dtypes

ORDER = 512
NT = 2048
NF = 256
DEV = 128
TR = 1024
F32 = jnp.float32
BF16 = jnp.bfloat16
I32 = jnp.int32
LIMIT = 56 * 1024 * 1024


def dft_tables():
    bins, freqs, part = np.meshgrid(np.arange(8), np.arange(16), np.arange(2), indexing="ij")
    first = freqs * 16 + bins * 2
    order = (1, 0, 2)
    freq = np.concatenate([first.reshape(-1), (first + 1).transpose(order).reshape(-1)])
    part = np.concatenate([part.reshape(-1), part.transpose(order).reshape(-1)])
    phase = (np.arange(NT)[:, None] * freq[None, :]) % NT
    angle = 2.0 * np.pi / NT * phase
    table = np.where(part[None, :] == 0, np.cos(angle), -np.sin(angle)) / math.sqrt(NT)
    high = table.astype(ml_dtypes.bfloat16)
    low = (table - high.astype(np.float64)).astype(ml_dtypes.bfloat16)
    return high, low


def index_kernel(rcv_ref, src_ref, order_ref, cell_ref, count_ref, start_ref, list_ref, edge_ref):
    lane = lax.broadcasted_iota(I32, (TR, DEV), 1)
    row_i = lax.broadcasted_iota(I32, (DEV, DEV), 0)
    col_i = lax.broadcasted_iota(I32, (DEV, DEV), 1)
    lower = (col_i < row_i).astype(BF16)
    upper = (row_i < col_i).astype(BF16)
    same = row_i == col_i
    rcv_cols, src_cols = [], []
    for blk in range(TR // DEV):
        for cols, ref in ((rcv_cols, rcv_ref), (src_cols, src_ref)):
            spread = jnp.where(same, jnp.broadcast_to(ref[blk : blk + 1, :], (DEV, DEV)), 0)
            cols.append(jnp.sum(spread.astype(F32), axis=1, keepdims=True).astype(I32))
    rcv = jnp.concatenate(rcv_cols, axis=0)
    src = jnp.concatenate(src_cols, axis=0)
    member = (rcv // 4 == lane).astype(F32)
    carry = jnp.zeros((1, DEV), F32)
    ranks = []
    for blk in range(TR // DEV):
        m = member[blk * DEV : (blk + 1) * DEV]
        ranks.append(jnp.dot(lower, m.astype(BF16), preferred_element_type=F32) + carry)
        carry = carry + jnp.sum(m, axis=0, keepdims=True)
    rank_all = jnp.concatenate(ranks, axis=0)
    counts8 = jnp.broadcast_to(carry, (8, DEV))
    start = jnp.dot(counts8.astype(BF16), upper, preferred_element_type=F32)
    place = jnp.sum(member * (rank_all + start[0:1]), axis=1, keepdims=True).astype(I32)
    order_ref[...] = place
    count_ref[...] = counts8.astype(I32)
    start_ref[...] = start.astype(I32)
    high = ((src // 128) * 4 + rcv % 4).astype(F32)
    low = (src % 128).astype(F32)
    digit = lax.broadcasted_iota(I32, (TR, DEV), 1)
    digits = jnp.where(digit == 0, high, jnp.where(digit == 1, low, 0.0)).astype(BF16)
    pick = (place == lax.broadcasted_iota(I32, (TR, TR), 1)).astype(F32).astype(BF16)
    both = lax.dot_general(digits, pick, (((0,), (0,)), ((), ())), preferred_element_type=F32)
    for blk in range(TR // DEV):
        cell_ref[blk : blk + 1, :] = both[0:1, blk * DEV : (blk + 1) * DEV]
        cell_ref[8 + blk : 9 + blk, :] = both[1:2, blk * DEV : (blk + 1) * DEV]
    cls = [carry <= 4.0, (carry > 4.0) & (carry <= 8.0), carry > 8.0]
    base = jnp.zeros((1, 1), F32)
    spot = jnp.zeros((1, DEV), F32)
    edges = []
    for kind in cls:
        ind = kind.astype(F32)
        before = jnp.dot(jnp.broadcast_to(ind, (8, DEV)).astype(BF16), upper, preferred_element_type=F32)[0:1]
        spot = spot + ind * (before + base)
        base = base + jnp.sum(ind, axis=1, keepdims=True)
        edges.append(base)
    here = (jnp.broadcast_to(spot, (DEV, DEV)) == row_i.astype(F32)).astype(BF16)
    names = lax.broadcasted_iota(I32, (8, DEV), 1).astype(F32).astype(BF16)
    list_ref[...] = lax.dot_general(
        names, here, (((1,), (1,)), ((), ())), preferred_element_type=F32
    ).astype(I32)
    edge_lane = lax.broadcasted_iota(I32, (8, DEV), 1)
    edge = jnp.where(edge_lane == 0, edges[0], jnp.where(edge_lane == 1, edges[1], edges[2]))
    edge_ref[...] = edge.astype(I32)


class Exchange:
    def __init__(self, axis, size, source, target, send, recv):
        self.axis, self.size, self.source, self.target = axis, size, source, target
        self.send, self.recv = send, recv
        self.me = lax.axis_index(axis)

    def copy(self, k):
        peer = lax.rem(self.me + k, self.size)
        return pltpu.make_async_remote_copy(
            src_ref=self.source(peer),
            dst_ref=self.target(self.me),
            send_sem=self.send.at[k],
            recv_sem=self.recv.at[k],
            device_id={self.axis: peer},
            device_id_type=pl.DeviceIdType.MESH,
        )

    def own(self):
        return pltpu.make_async_copy(self.source(self.me), self.target(self.me), self.recv.at[0])

    def start(self):
        def step(k, _):
            self.copy(k).start()
            return 0

        lax.fori_loop(1, self.size, step, 0)
        self.own().start()

    def wait_recv(self):
        def step(k, _):
            self.copy(k).wait_recv()
            return 0

        lax.fori_loop(1, self.size, step, 0)
        self.own().wait()

    def wait_send(self):
        def step(k, _):
            self.copy(k).wait_send()
            return 0

        lax.fori_loop(1, self.size, step, 0)


def greet(axes):
    barrier = pltpu.get_barrier_semaphore()
    for axis, size in axes:
        me = lax.axis_index(axis)

        def step(k, _, axis=axis, size=size, me=me):
            pl.semaphore_signal(
                barrier, inc=1, device_id={axis: lax.rem(me + k, size)}, device_id_type=pl.DeviceIdType.MESH
            )
            return 0

        lax.fori_loop(1, size, step, 0)


def spectrum_kernel(
    steps,
    traces_ref,
    high_ref,
    low_ref,
    order_ref,
    cell_ref,
    data_ref,
    cells_ref,
    acc_ref,
    pick_ref,
    spread_ref,
    cell_send,
    cell_mid,
    first_send,
    first_mid,
    second_send,
    second_mid,
    bin_send,
    bin_recv,
    freq_send,
    freq_recv,
):
    step = pl.program_id(0)

    def over_bin(slot, source, target):
        return Exchange("bin", 8, source, target, bin_send.at[slot], bin_recv.at[slot])

    def over_freq(slot, source, target):
        return Exchange("freq", 16, source, target, freq_send.at[slot], freq_recv.at[slot])

    cell_bin = over_bin(0, lambda b: cell_send, lambda me: cell_mid.at[me])
    cell_freq = over_freq(0, lambda f: cell_mid, lambda me: cells_ref.at[:, me])
    first_bin = over_bin(1, lambda b: first_send.at[b], lambda me: first_mid.at[me])
    first_freq = over_freq(1, lambda f: first_mid.at[:, f], lambda me: data_ref.at[:, me, 0])
    second_freq = over_freq(2, lambda f: second_send.at[f], lambda me: second_mid.at[me])
    second_bin = over_bin(2, lambda b: second_mid.at[:, b], lambda me: data_ref.at[me, :, 1])

    @pl.when(step == 0)
    def _():
        greet((("bin", 8), ("freq", 16)))
        acc_ref[...] = jnp.zeros_like(acc_ref)
        cell_send[...] = cell_ref[...].astype(BF16)
        pick_ref[...] = (order_ref[...] == lax.broadcasted_iota(I32, (TR, TR), 1)).astype(F32).astype(BF16)

    @pl.when(step == 1)
    def _():
        pl.semaphore_wait(pltpu.get_barrier_semaphore(), 22)
        cell_bin.start()

    @pl.when(step == 2)
    def _():
        cell_bin.wait_recv()
        cell_freq.start()

    x = traces_ref[...]
    acc_ref[...] += jnp.dot(x, high_ref[...], preferred_element_type=F32) + jnp.dot(
        x, low_ref[...], preferred_element_type=F32
    )

    @pl.when(step == steps - 1)
    def _():
        def sorted_rows(half):
            spec = acc_ref[:, half * 256 : (half + 1) * 256].astype(BF16)
            rows = lax.dot_general(
                spec, pick_ref[...], (((0,), (0,)), ((), ())), preferred_element_type=F32
            )
            for blk in range(8):
                spread_ref[pl.ds(blk, 256, stride=8), :] = rows[:, blk * DEV : (blk + 1) * DEV]

        sorted_rows(0)
        for b in range(8):
            first_send[b] = spread_ref[b * 256 : (b + 1) * 256, :].reshape(16, 16, DEV).astype(BF16)
        first_bin.start()
        sorted_rows(1)
        for f in range(16):
            second_send[f] = spread_ref[f * 128 : (f + 1) * 128, :].reshape(8, 16, DEV).astype(BF16)
        second_freq.start()
        first_bin.wait_recv()
        first_freq.start()
        second_freq.wait_recv()
        second_bin.start()
        cell_freq.wait_recv()
        first_freq.wait_recv()
        second_bin.wait_recv()
        for part in (cell_bin, cell_freq, first_bin, first_freq, second_freq, second_bin):
            part.wait_send()


def layout_kernel(
    count_ref, start_ref, list_ref, edge_ref, data_ref, code_ref, dense_ref, wide_ref, rows_ref, cell_ref, raw_ref
):
    stride = TR + 16
    for b in range(8):
        wide_ref[b * 512 : (b + 1) * 512, :] = data_ref[b].reshape(512, DEV).astype(F32)
        cell_wide = code_ref[b].reshape(256, DEV).astype(F32)
        wide_ref[4096 + b * 256 : 4096 + (b + 1) * 256, :] = cell_wide
    for blk in range(8):
        for comp in range(4):
            rows_ref[pl.ds(comp * stride + blk * DEV, DEV), :] = wide_ref[pl.ds(comp * 8 + blk, DEV, stride=32), :].T
        for digit in range(2):
            cell_ref[pl.ds(digit * stride + blk * DEV, DEV), :] = wide_ref[
                pl.ds(4096 + digit * 8 + blk, DEV, stride=16), :
            ].T
    pad = jnp.zeros((16, DEV), F32)
    for comp in range(4):
        rows_ref[pl.ds(comp * stride + TR, 16), :] = pad
    for digit in range(2):
        cell_ref[pl.ds(digit * stride + TR, 16), :] = pad

    sub16 = lax.broadcasted_iota(I32, (16, DEV), 0).astype(F32)
    sub128 = lax.broadcasted_iota(I32, (DEV, DEV), 0).astype(F32).astype(BF16)
    one, zero = jnp.ones((), BF16), jnp.zeros((), BF16)

    def lay_out(run, size):
        count = count_ref[0, run]
        start = start_ref[0, run]
        left, right = [], []
        for j in range(size):
            at = start + j
            high = jnp.broadcast_to(cell_ref[pl.ds(at, 1), :], (16, DEV))
            hit = jnp.where(j < count, high, -1.0) == sub16
            parts = []
            for comp in range(4):
                row = jnp.broadcast_to(rows_ref[pl.ds(comp * stride + at, 1), :], (16, DEV))
                parts.append(jnp.where(hit, row, 0.0).astype(BF16))
            left.append(jnp.concatenate(parts, axis=0))
            low = jnp.broadcast_to(cell_ref[pl.ds(stride + at, 1), :], (16, DEV)).astype(BF16)
            right.append(jnp.where(jnp.concatenate([low] * 8, axis=0) == sub128, one, zero))
        raw_ref[run] = lax.dot_general(
            jnp.concatenate(left, axis=1),
            jnp.concatenate(right, axis=1),
            (((1,), (1,)), ((), ())),
            preferred_element_type=F32,
        )

    begin = 0
    for kind, (size, together) in enumerate(((4, 4), (8, 4), (16, 2))):
        end = edge_ref[0, kind]

        def some_runs(step, _, begin=begin, end=end, size=size, together=together):
            for u in range(together):
                lay_out(list_ref[0, jnp.minimum(begin + step * together + u, end - 1)], size)
            return 0

        lax.fori_loop(0, (end - begin + together - 1) // together, some_runs, 0)
        begin = end

    top = lax.broadcasted_iota(I32, (8, DEV), 0) < 4

    def four_runs(group, _):
        for comp in range(4):
            at = pl.ds(pl.multiple_of(comp * ORDER + group * 16, 16), 16)
            for v in range(2):
                sl = pl.ds(comp * 16 + 8 * v, 8)
                a, b, c, d = [raw_ref[4 * group + u, sl, :] for u in range(4)]
                first = [jnp.where(top, a, pltpu.roll(b, 4, 0)), jnp.where(top, c, pltpu.roll(d, 4, 0))]
                last = [jnp.where(top, pltpu.roll(a, 4, 0), b), jnp.where(top, pltpu.roll(c, 4, 0), d)]
                dense_ref[at, pl.ds(2 * v * DEV, DEV)] = jnp.concatenate(first, axis=0).astype(BF16)
                dense_ref[at, pl.ds((2 * v + 1) * DEV, DEV)] = jnp.concatenate(last, axis=0).astype(BF16)
        return 0

    lax.fori_loop(0, DEV // 4, four_runs, 0, unroll=2)


def product_kernel(filt_ref, dense_ref, out_ref, block_ref, send, recv):
    mine = lax.axis_index("bin") * 2
    amplitude = 1.0 / math.sqrt(ORDER)
    greet((("bin", 8),))
    moves = [
        Exchange(
            "bin",
            8,
            lambda b, i=i: block_ref.at[b, i],
            lambda me, i=i: out_ref.at[:, me * 2 + i],
            send.at[i],
            recv.at[i],
        )
        for i in range(2)
    ]
    for i in range(2):
        real = dense_ref[pl.ds(2 * i * ORDER, ORDER), :]
        imag = dense_ref[pl.ds((2 * i + 1) * ORDER, ORDER), :]
        fr = filt_ref[0, mine + i]
        fi = filt_ref[1, mine + i]
        for t in range(2):
            cols = slice(t * 256, (t + 1) * 256)
            rc, ic = real[:, cols], imag[:, cols]
            dot = functools.partial(jnp.dot, preferred_element_type=F32)
            sr = dot(real, rc) - dot(imag, ic)
            si = dot(real, ic) + dot(imag, rc)
            outr = ((fr * sr - fi * si) * amplitude).astype(BF16)
            outi = ((fr * si + fi * sr) * amplitude).astype(BF16)
            for b in range(8):
                block_ref[b, i, 0, :, cols] = outr[b * 64 : (b + 1) * 64]
                block_ref[b, i, 1, :, cols] = outi[b * 64 : (b + 1) * 64]
        if i == 0:
            pl.semaphore_wait(pltpu.get_barrier_semaphore(), 7)
        moves[i].start()
    for move in moves:
        move.wait_recv()
        move.wait_send()


def local(traces, rcv_index, src_index, wave_filter):
    high, low = dft_tables()
    params = pltpu.CompilerParams(vmem_limit_bytes=LIMIT)
    vmem = pl.BlockSpec(memory_space=pltpu.VMEM)
    smem = pl.BlockSpec(memory_space=pltpu.SMEM)
    anywhere = pl.BlockSpec(memory_space=pl.ANY)
    shape = jax.ShapeDtypeStruct
    small = shape((8, DEV), I32)
    order, cells, count, start, listed, edge = pl.pallas_call(
        index_kernel,
        out_shape=(shape((TR, 1), I32), shape((16, DEV), F32), small, small, small, small),
        compiler_params=params,
        name="index",
    )(rcv_index.reshape(8, DEV), src_index.reshape(8, DEV))
    steps = 4
    depth = NT // steps
    dma = pltpu.SemaphoreType.DMA
    data, cells = pl.pallas_call(
        functools.partial(spectrum_kernel, steps),
        grid=(steps,),
        in_specs=[
            pl.BlockSpec((TR, depth), lambda k: (0, k)),
            pl.BlockSpec((depth, 4 * DEV), lambda k: (k, 0)),
            pl.BlockSpec((depth, 4 * DEV), lambda k: (k, 0)),
            pl.BlockSpec((TR, 1), lambda k: (0, 0)),
            pl.BlockSpec((16, DEV), lambda k: (0, 0)),
        ],
        out_specs=(anywhere, anywhere),
        out_shape=(shape((8, 16, 2, 16, DEV), BF16), shape((8, 16, 16, DEV), BF16)),
        scratch_shapes=[
            pltpu.VMEM((TR, 4 * DEV), F32),
            pltpu.VMEM((TR, TR), BF16),
            pltpu.VMEM((2048, DEV), F32),
            pltpu.VMEM((16, DEV), BF16),
            pltpu.VMEM((8, 16, DEV), BF16),
            pltpu.VMEM((8, 16, 16, DEV), BF16),
            pltpu.VMEM((8, 16, 16, DEV), BF16),
            pltpu.VMEM((16, 8, 16, DEV), BF16),
            pltpu.VMEM((16, 8, 16, DEV), BF16),
            dma((3, 8)),
            dma((3, 8)),
            dma((3, 16)),
            dma((3, 16)),
        ],
        compiler_params=pltpu.CompilerParams(vmem_limit_bytes=LIMIT, collective_id=1, has_side_effects=True),
        cost_estimate=pl.CostEstimate(flops=5 * 10**9, bytes_accessed=9 * 10**6, transcendentals=0),
        name="spectrum",
    )(traces, jnp.asarray(high), jnp.asarray(low), order, cells)
    dense = pl.pallas_call(
        layout_kernel,
        in_specs=[smem, smem, smem, smem, vmem, vmem],
        out_specs=vmem,
        out_shape=shape((4 * ORDER, ORDER), BF16),
        scratch_shapes=[
            pltpu.VMEM((4096 + 2048, DEV), F32),
            pltpu.VMEM((4 * (TR + 16), DEV), F32),
            pltpu.VMEM((2 * (TR + 16), DEV), F32),
            pltpu.VMEM((DEV, 64, DEV), F32),
        ],
        compiler_params=params,
        name="layout",
    )(count, start, listed, edge, data, cells)
    return pl.pallas_call(
        product_kernel,
        in_specs=[smem, vmem],
        out_specs=anywhere,
        out_shape=shape((2, 16, 64, ORDER), BF16),
        scratch_shapes=[pltpu.VMEM((8, 2, 2, 64, ORDER), BF16), dma((2, 8)), dma((2, 8))],
        compiler_params=pltpu.CompilerParams(vmem_limit_bytes=LIMIT, collective_id=2, has_side_effects=True),
        name="product",
    )(wave_filter, dense)


def solution(mesh):
    placed = (P(("bin", "freq"), None), P(("bin", "freq")), P(("bin", "freq")), P(None, "freq"))
    return jax.shard_map(
        local, mesh=mesh, in_specs=placed, out_specs=P(None, "freq", "bin", None), check_vma=False
    )
```

```python
import functools
import math

import jax
import jax.numpy as jnp
import numpy as np
from jax import lax
from jax.experimental import pallas as pl
from jax.experimental.pallas import tpu as pltpu
from jax.sharding import PartitionSpec as P
import ml_dtypes

ORDER = 512
NT = 2048
NF = 256
DEV = 128
TR = 1024
F32 = jnp.float32
BF16 = jnp.bfloat16
I32 = jnp.int32
LIMIT = 56 * 1024 * 1024


def dft_tables():
    bins, freqs, part = np.meshgrid(np.arange(8), np.arange(16), np.arange(2), indexing="ij")
    first = freqs * 16 + bins * 2
    order = (1, 0, 2)
    freq = np.concatenate([first.reshape(-1), (first + 1).transpose(order).reshape(-1)])
    part = np.concatenate([part.reshape(-1), part.transpose(order).reshape(-1)])
    phase = (np.arange(NT)[:, None] * freq[None, :]) % NT
    angle = 2.0 * np.pi / NT * phase
    table = np.where(part[None, :] == 0, np.cos(angle), -np.sin(angle)) / math.sqrt(NT)
    high = table.astype(ml_dtypes.bfloat16)
    low = (table - high.astype(np.float64)).astype(ml_dtypes.bfloat16)
    return [np.concatenate([high[:, h : h + 256], low[:, h : h + 256]], axis=1) for h in (0, 256)]


def index_work(rcv_ref, src_ref, pick_ref, cell_ref, spread_ref, count_ref, start_ref):
    lane = lax.broadcasted_iota(I32, (TR, DEV), 1)
    row_i = lax.broadcasted_iota(I32, (DEV, DEV), 0)
    col_i = lax.broadcasted_iota(I32, (DEV, DEV), 1)
    lower = (col_i < row_i).astype(BF16)
    upper = (row_i < col_i).astype(BF16)
    same = row_i == col_i
    rcv_cols, src_cols = [], []
    for blk in range(TR // DEV):
        for cols, ref in ((rcv_cols, rcv_ref), (src_cols, src_ref)):
            spread = jnp.where(same, jnp.broadcast_to(ref[blk : blk + 1, :], (DEV, DEV)), 0)
            cols.append(jnp.sum(spread.astype(F32), axis=1, keepdims=True).astype(I32))
    rcv = jnp.concatenate(rcv_cols, axis=0)
    src = jnp.concatenate(src_cols, axis=0)
    member = (rcv // 4 == lane).astype(F32)
    carry = jnp.zeros((1, DEV), F32)
    ranks = []
    for blk in range(TR // DEV):
        m = member[blk * DEV : (blk + 1) * DEV]
        ranks.append(jnp.dot(lower, m.astype(BF16), preferred_element_type=F32) + carry)
        carry = carry + jnp.sum(m, axis=0, keepdims=True)
    rank_all = jnp.concatenate(ranks, axis=0)
    counts8 = jnp.broadcast_to(carry, (8, DEV))
    start = jnp.dot(counts8.astype(BF16), upper, preferred_element_type=F32)
    place = jnp.sum(member * (rank_all + start[0:1]), axis=1, keepdims=True).astype(I32)
    count_ref[...] = counts8.astype(I32)
    start_ref[...] = start.astype(I32)
    high = ((src // 128) * 4 + rcv % 4).astype(F32)
    low = (src % 128).astype(F32)
    digit = lax.broadcasted_iota(I32, (TR, DEV), 1)
    digits = jnp.where(digit == 0, high, jnp.where(digit == 1, low, 0.0)).astype(BF16)
    pick_ref[...] = (place == lax.broadcasted_iota(I32, (TR, TR), 1)).astype(F32).astype(BF16)
    both = lax.dot_general(digits, pick_ref[...], (((0,), (0,)), ((), ())), preferred_element_type=F32)
    for blk in range(TR // DEV):
        spread_ref[blk : blk + 1, :] = both[0:1, blk * DEV : (blk + 1) * DEV]
        spread_ref[8 + blk : 9 + blk, :] = both[1:2, blk * DEV : (blk + 1) * DEV]
    cell_ref[...] = spread_ref[0:16, :].astype(BF16)
    return carry, upper, row_i


def list_runs(carry, upper, row_i, list_ref, edge_ref):
    cls = [carry <= 4.0, (carry > 4.0) & (carry <= 8.0), carry > 8.0]
    base = jnp.zeros((1, 1), F32)
    spot = jnp.zeros((1, DEV), F32)
    edges = []
    for kind in cls:
        ind = kind.astype(F32)
        before = jnp.dot(jnp.broadcast_to(ind, (8, DEV)).astype(BF16), upper, preferred_element_type=F32)[0:1]
        spot = spot + ind * (before + base)
        base = base + jnp.sum(ind, axis=1, keepdims=True)
        edges.append(base)
    here = (jnp.broadcast_to(spot, (DEV, DEV)) == row_i.astype(F32)).astype(BF16)
    names = lax.broadcasted_iota(I32, (8, DEV), 1).astype(F32).astype(BF16)
    list_ref[...] = lax.dot_general(
        names, here, (((1,), (1,)), ((), ())), preferred_element_type=F32
    ).astype(I32)
    edge_lane = lax.broadcasted_iota(I32, (8, DEV), 1)
    edge = jnp.where(edge_lane == 0, edges[0], jnp.where(edge_lane == 1, edges[1], edges[2]))
    edge_ref[...] = edge.astype(I32)


class Exchange:
    def __init__(self, axis, size, source, target, send, recv):
        self.axis, self.size, self.source, self.target = axis, size, source, target
        self.send, self.recv = send, recv
        self.me = lax.axis_index(axis)

    def copy(self, k):
        peer = lax.rem(self.me + k, self.size)
        return pltpu.make_async_remote_copy(
            src_ref=self.source(peer),
            dst_ref=self.target(self.me),
            send_sem=self.send.at[k],
            recv_sem=self.recv.at[k],
            device_id={self.axis: peer},
            device_id_type=pl.DeviceIdType.MESH,
        )

    def own(self):
        return pltpu.make_async_copy(self.source(self.me), self.target(self.me), self.recv.at[0])

    def start(self):
        def step(k, _):
            self.copy(k).start()
            return 0

        lax.fori_loop(1, self.size, step, 0)
        self.own().start()

    def wait_recv(self):
        def step(k, _):
            self.copy(k).wait_recv()
            return 0

        lax.fori_loop(1, self.size, step, 0)
        self.own().wait()

    def wait_send(self):
        def step(k, _):
            self.copy(k).wait_send()
            return 0

        lax.fori_loop(1, self.size, step, 0)


def greet(axes):
    barrier = pltpu.get_barrier_semaphore()
    for axis, size in axes:
        me = lax.axis_index(axis)

        def step(k, _, axis=axis, size=size, me=me):
            pl.semaphore_signal(
                barrier, inc=1, device_id={axis: lax.rem(me + k, size)}, device_id_type=pl.DeviceIdType.MESH
            )
            return 0

        lax.fori_loop(1, size, step, 0)


def spectrum_kernel(
    rcv_ref,
    src_ref,
    traces_ref,
    first_ref,
    second_ref,
    data_first_ref,
    data_second_ref,
    cells_ref,
    count_ref,
    start_ref,
    list_ref,
    edge_ref,
    x_ref,
    table_ref,
    pick_ref,
    spec_ref,
    spread_ref,
    cell_send,
    cell_mid,
    first_send,
    first_mid,
    second_send,
    second_mid,
    load_sem,
    bin_send,
    bin_recv,
    freq_send,
    freq_recv,
):
    def over_bin(slot, source, target):
        return Exchange("bin", 8, source, target, bin_send.at[slot], bin_recv.at[slot])

    def over_freq(slot, source, target):
        return Exchange("freq", 16, source, target, freq_send.at[slot], freq_recv.at[slot])

    cell_bin = over_bin(0, lambda b: cell_send, lambda me: cell_mid.at[me])
    cell_freq = over_freq(0, lambda f: cell_mid, lambda me: cells_ref.at[me])
    first_bin = over_bin(1, lambda b: first_send.at[b], lambda me: first_mid.at[me])
    first_freq = over_freq(1, lambda f: first_mid.at[:, f], lambda me: data_first_ref.at[me])
    second_freq = over_freq(2, lambda f: second_send.at[f], lambda me: second_mid.at[me])
    second_bin = over_bin(2, lambda b: second_mid.at[:, b], lambda me: data_second_ref.at[me])

    def load_traces(m):
        at = pl.ds(m * 256, 256)
        return pltpu.make_async_copy(traces_ref.at[at], x_ref.at[at], load_sem.at[m])

    def load_table(h):
        return pltpu.make_async_copy((first_ref, second_ref)[h], table_ref.at[h], load_sem.at[4 + h])

    greet((("bin", 8), ("freq", 16)))
    load_table(0).start()
    for m in range(4):
        load_traces(m).start()
    load_table(1).start()
    carry, upper, row_i = index_work(rcv_ref, src_ref, pick_ref, cell_send, spread_ref, count_ref, start_ref)
    pl.semaphore_wait(pltpu.get_barrier_semaphore(), 22)
    cell_bin.start()
    list_runs(carry, upper, row_i, list_ref, edge_ref)

    def transform(h):
        load_table(h).wait()

        def rows(m, _):
            if h == 0:
                load_traces(m).wait()
            at = pl.ds(pl.multiple_of(m * 256, 256), 256)
            both = jnp.dot(x_ref[at, :], table_ref[h], preferred_element_type=F32)
            spec_ref[at, :] = (both[:, :256] + both[:, 256:]).astype(BF16)
            return 0

        lax.fori_loop(0, 4, rows, 0)

    def sort_rows():
        for half in range(2):
            q = half * 512
            rows = lax.dot_general(
                spec_ref[...], pick_ref[:, q : q + 512], (((0,), (0,)), ((), ())), preferred_element_type=F32
            )
            for blk in range(4):
                spread_ref[pl.ds(half * 4 + blk, 256, stride=8), :] = rows[:, blk * DEV : (blk + 1) * DEV]

    transform(0)
    cell_bin.wait_recv()
    cell_freq.start()
    sort_rows()
    for b in range(8):
        first_send[b] = spread_ref[b * 256 : (b + 1) * 256, :].reshape(16, 16, DEV).astype(BF16)
    first_bin.start()
    transform(1)
    sort_rows()
    for f in range(16):
        second_send[f] = spread_ref[f * 128 : (f + 1) * 128, :].reshape(8, 16, DEV).astype(BF16)
    second_freq.start()
    first_bin.wait_recv()
    first_freq.start()
    second_freq.wait_recv()
    second_bin.start()
    cell_freq.wait_recv()
    first_freq.wait_recv()
    second_bin.wait_recv()
    for part in (cell_bin, cell_freq, first_bin, first_freq, second_freq, second_bin):
        part.wait_send()


def layout_kernel(
    count_ref,
    start_ref,
    list_ref,
    edge_ref,
    first_ref,
    second_ref,
    code_ref,
    dense_ref,
    first_wide,
    second_wide,
    code_wide,
    rows_ref,
    cell_ref,
    raw_ref,
):
    stride = TR + 16
    for b in range(8):
        second_wide[b * 256 : (b + 1) * 256, :] = second_ref[b].reshape(256, DEV).astype(F32)
        for f in range(16):
            at = (b * 16 + f) * 16
            first_wide[at : at + 16, :] = first_ref[f, b].astype(F32)
            code_wide[at : at + 16, :] = code_ref[f, b].astype(F32)
    for blk in range(8):
        for part in range(2):
            pick = pl.ds(part * 8 + blk, DEV, stride=16)
            rows_ref[pl.ds(part * stride + blk * DEV, DEV), :] = first_wide[pick, :].T
            rows_ref[pl.ds((2 + part) * stride + blk * DEV, DEV), :] = second_wide[pick, :].T
            cell_ref[pl.ds(part * stride + blk * DEV, DEV), :] = code_wide[pick, :].T
    pad = jnp.zeros((16, DEV), F32)
    for comp in range(4):
        rows_ref[pl.ds(comp * stride + TR, 16), :] = pad
    for digit in range(2):
        cell_ref[pl.ds(digit * stride + TR, 16), :] = pad

    sub16 = lax.broadcasted_iota(I32, (16, DEV), 0).astype(F32)
    sub128 = lax.broadcasted_iota(I32, (DEV, DEV), 0).astype(F32).astype(BF16)
    one, zero = jnp.ones((), BF16), jnp.zeros((), BF16)

    def lay_out(run, size):
        count = count_ref[0, run]
        start = start_ref[0, run]
        left, right = [], []
        for j in range(size):
            at = start + j
            high = jnp.broadcast_to(cell_ref[pl.ds(at, 1), :], (16, DEV))
            hit = jnp.where(j < count, high, -1.0) == sub16
            parts = []
            for comp in range(4):
                row = jnp.broadcast_to(rows_ref[pl.ds(comp * stride + at, 1), :], (16, DEV))
                parts.append(jnp.where(hit, row, 0.0).astype(BF16))
            left.append(jnp.concatenate(parts, axis=0))
            low = jnp.broadcast_to(cell_ref[pl.ds(stride + at, 1), :], (16, DEV)).astype(BF16)
            right.append(jnp.where(jnp.concatenate([low] * 8, axis=0) == sub128, one, zero))
        raw_ref[run] = lax.dot_general(
            jnp.concatenate(left, axis=1),
            jnp.concatenate(right, axis=1),
            (((1,), (1,)), ((), ())),
            preferred_element_type=F32,
        )

    begin = 0
    for kind, (size, together) in enumerate(((4, 4), (8, 4), (16, 2))):
        end = edge_ref[0, kind]

        def some_runs(step, _, begin=begin, end=end, size=size, together=together):
            for u in range(together):
                lay_out(list_ref[0, jnp.minimum(begin + step * together + u, end - 1)], size)
            return 0

        lax.fori_loop(0, (end - begin + together - 1) // together, some_runs, 0)
        begin = end

    top = lax.broadcasted_iota(I32, (8, DEV), 0) < 4

    def four_runs(group, _):
        for comp in range(4):
            at = pl.ds(pl.multiple_of(comp * ORDER + group * 16, 16), 16)
            for v in range(2):
                sl = pl.ds(comp * 16 + 8 * v, 8)
                a, b, c, d = [raw_ref[4 * group + u, sl, :] for u in range(4)]
                first = [jnp.where(top, a, pltpu.roll(b, 4, 0)), jnp.where(top, c, pltpu.roll(d, 4, 0))]
                last = [jnp.where(top, pltpu.roll(a, 4, 0), b), jnp.where(top, pltpu.roll(c, 4, 0), d)]
                dense_ref[at, pl.ds(2 * v * DEV, DEV)] = jnp.concatenate(first, axis=0).astype(BF16)
                dense_ref[at, pl.ds((2 * v + 1) * DEV, DEV)] = jnp.concatenate(last, axis=0).astype(BF16)
        return 0

    lax.fori_loop(0, DEV // 4, four_runs, 0, unroll=2)


def product_kernel(filt_ref, dense_ref, out_ref, block_ref, send, recv):
    mine = lax.axis_index("bin") * 2
    amplitude = 1.0 / math.sqrt(ORDER)
    greet((("bin", 8),))
    moves = [
        Exchange(
            "bin",
            8,
            lambda b, i=i: block_ref.at[b, i],
            lambda me, i=i: out_ref.at[:, me * 2 + i],
            send.at[i],
            recv.at[i],
        )
        for i in range(2)
    ]
    for i in range(2):
        real = dense_ref[pl.ds(2 * i * ORDER, ORDER), :]
        imag = dense_ref[pl.ds((2 * i + 1) * ORDER, ORDER), :]
        fr = filt_ref[0, mine + i]
        fi = filt_ref[1, mine + i]
        for t in range(2):
            cols = slice(t * 256, (t + 1) * 256)
            rc, ic = real[:, cols], imag[:, cols]
            dot = functools.partial(jnp.dot, preferred_element_type=F32)
            sr = dot(real, rc) - dot(imag, ic)
            si = dot(real, ic) + dot(imag, rc)
            outr = ((fr * sr - fi * si) * amplitude).astype(BF16)
            outi = ((fr * si + fi * sr) * amplitude).astype(BF16)
            for b in range(8):
                block_ref[b, i, 0, :, cols] = outr[b * 64 : (b + 1) * 64]
                block_ref[b, i, 1, :, cols] = outi[b * 64 : (b + 1) * 64]
        if i == 0:
            pl.semaphore_wait(pltpu.get_barrier_semaphore(), 7)
        moves[i].start()
    for move in moves:
        move.wait_recv()
        move.wait_send()


def local(traces, rcv_index, src_index, wave_filter):
    tables = dft_tables()
    params = pltpu.CompilerParams(vmem_limit_bytes=LIMIT)
    vmem = pl.BlockSpec(memory_space=pltpu.VMEM)
    smem = pl.BlockSpec(memory_space=pltpu.SMEM)
    anywhere = pl.BlockSpec(memory_space=pl.ANY)
    shape = jax.ShapeDtypeStruct
    small = shape((8, DEV), I32)
    dma = pltpu.SemaphoreType.DMA
    outgoing, middle = pltpu.VMEM((8, 16, 16, DEV), BF16), pltpu.VMEM((16, 8, 16, DEV), BF16)
    first, second, cells, count, start, listed, edge = pl.pallas_call(
        spectrum_kernel,
        in_specs=[vmem, vmem, anywhere, anywhere, anywhere],
        out_specs=(anywhere, anywhere, anywhere, vmem, vmem, vmem, vmem),
        out_shape=(
            shape((16, 8, 16, DEV), BF16),
            shape((8, 16, 16, DEV), BF16),
            shape((16, 8, 16, DEV), BF16),
            small,
            small,
            small,
            small,
        ),
        scratch_shapes=[
            pltpu.VMEM((TR, NT), BF16),
            pltpu.VMEM((2, NT, 4 * DEV), BF16),
            pltpu.VMEM((TR, TR), BF16),
            pltpu.VMEM((TR, 256), BF16),
            pltpu.VMEM((2048, DEV), F32),
            pltpu.VMEM((16, DEV), BF16),
            pltpu.VMEM((8, 16, DEV), BF16),
            outgoing,
            outgoing,
            middle,
            middle,
            dma((6,)),
            dma((3, 8)),
            dma((3, 8)),
            dma((3, 16)),
            dma((3, 16)),
        ],
        compiler_params=pltpu.CompilerParams(vmem_limit_bytes=LIMIT, collective_id=1, has_side_effects=True),
        cost_estimate=pl.CostEstimate(flops=5 * 10**9, bytes_accessed=9 * 10**6, transcendentals=0),
        name="spectrum",
    )(rcv_index.reshape(8, DEV), src_index.reshape(8, DEV), traces, jnp.asarray(tables[0]), jnp.asarray(tables[1]))
    dense = pl.pallas_call(
        layout_kernel,
        in_specs=[smem, smem, smem, smem, vmem, vmem, vmem],
        out_specs=vmem,
        out_shape=shape((4 * ORDER, ORDER), BF16),
        scratch_shapes=[
            pltpu.VMEM((2048, DEV), F32),
            pltpu.VMEM((2048, DEV), F32),
            pltpu.VMEM((2048, DEV), F32),
            pltpu.VMEM((4 * (TR + 16), DEV), F32),
            pltpu.VMEM((2 * (TR + 16), DEV), F32),
            pltpu.VMEM((DEV, 64, DEV), F32),
        ],
        compiler_params=params,
        name="layout",
    )(count, start, listed, edge, first, second, cells)
    return pl.pallas_call(
        product_kernel,
        in_specs=[smem, vmem],
        out_specs=anywhere,
        out_shape=shape((2, 16, 64, ORDER), BF16),
        scratch_shapes=[pltpu.VMEM((8, 2, 2, 64, ORDER), BF16), dma((2, 8)), dma((2, 8))],
        compiler_params=pltpu.CompilerParams(vmem_limit_bytes=LIMIT, collective_id=2, has_side_effects=True),
        name="product",
    )(wave_filter, dense)


def solution(mesh):
    placed = (P(("bin", "freq"), None), P(("bin", "freq")), P(("bin", "freq")), P(None, "freq"))
    return jax.shard_map(
        local, mesh=mesh, in_specs=placed, out_specs=P(None, "freq", "bin", None), check_vma=False
    )
```

```python
import functools
import math

import jax
import jax.numpy as jnp
import numpy as np
from jax import lax
from jax.experimental import pallas as pl
from jax.experimental.pallas import tpu as pltpu
from jax.sharding import PartitionSpec as P
import ml_dtypes

ORDER = 512
NT = 2048
NF = 256
DEV = 128
TR = 1024
F32 = jnp.float32
BF16 = jnp.bfloat16
I32 = jnp.int32
LIMIT = 56 * 1024 * 1024


def dft_tables():
    bins, freqs, part = np.meshgrid(np.arange(8), np.arange(16), np.arange(2), indexing="ij")
    first = freqs * 16 + bins * 2
    order = (1, 0, 2)
    freq = np.concatenate([first.reshape(-1), (first + 1).transpose(order).reshape(-1)])
    part = np.concatenate([part.reshape(-1), part.transpose(order).reshape(-1)])
    phase = (np.arange(NT)[:, None] * freq[None, :]) % NT
    angle = 2.0 * np.pi / NT * phase
    table = np.where(part[None, :] == 0, np.cos(angle), -np.sin(angle)) / math.sqrt(NT)
    high = table.astype(ml_dtypes.bfloat16)
    low = (table - high.astype(np.float64)).astype(ml_dtypes.bfloat16)
    return [np.concatenate([high[:, h : h + 256], low[:, h : h + 256]], axis=1) for h in (0, 256)]


def index_work(rcv_ref, src_ref, pick_ref, cell_ref, count_ref, start_ref):
    lane = lax.broadcasted_iota(I32, (TR, DEV), 1)
    row_i = lax.broadcasted_iota(I32, (DEV, DEV), 0)
    col_i = lax.broadcasted_iota(I32, (DEV, DEV), 1)
    lower = (col_i < row_i).astype(BF16)
    upper = (row_i < col_i).astype(BF16)
    same = row_i == col_i
    rcv_cols, src_cols = [], []
    for blk in range(TR // DEV):
        for cols, ref in ((rcv_cols, rcv_ref), (src_cols, src_ref)):
            spread = jnp.where(same, jnp.broadcast_to(ref[blk : blk + 1, :], (DEV, DEV)), 0)
            cols.append(jnp.sum(spread.astype(F32), axis=1, keepdims=True).astype(I32))
    rcv = jnp.concatenate(rcv_cols, axis=0)
    src = jnp.concatenate(src_cols, axis=0)
    member = (rcv // 4 == lane).astype(F32)
    carry = jnp.zeros((1, DEV), F32)
    ranks = []
    for blk in range(TR // DEV):
        m = member[blk * DEV : (blk + 1) * DEV]
        ranks.append(jnp.dot(lower, m.astype(BF16), preferred_element_type=F32) + carry)
        carry = carry + jnp.sum(m, axis=0, keepdims=True)
    rank_all = jnp.concatenate(ranks, axis=0)
    counts8 = jnp.broadcast_to(carry, (8, DEV))
    start = jnp.dot(counts8.astype(BF16), upper, preferred_element_type=F32)
    place = jnp.sum(member * (rank_all + start[0:1]), axis=1, keepdims=True).astype(I32)
    count_ref[...] = counts8.astype(I32)
    start_ref[...] = start.astype(I32)
    half = (src // 64 + rcv // 4) % 2
    high = ((src // 128) * 8 + half * 4 + rcv % 4).astype(F32)
    low = (src % 64).astype(F32)
    digit = lax.broadcasted_iota(I32, (TR, DEV), 1)
    digits = jnp.where(digit == 0, high, jnp.where(digit == 1, low, 0.0)).astype(BF16)
    pick_ref[...] = (place == lax.broadcasted_iota(I32, (TR, TR), 1)).astype(F32).astype(BF16)
    both = lax.dot_general(digits, pick_ref[...], (((0,), (0,)), ((), ())), preferred_element_type=F32)
    for blk in range(TR // DEV):
        cols = slice(blk * DEV, (blk + 1) * DEV)
        cell_ref[blk : blk + 1, :] = (both[0:1, cols] * 64.0 + both[1:2, cols]).astype(I32)
    return carry, upper, row_i


def list_runs(carry, upper, row_i, list_ref, edge_ref):
    cls = [carry <= 4.0, (carry > 4.0) & (carry <= 8.0), carry > 8.0]
    base = jnp.zeros((1, 1), F32)
    spot = jnp.zeros((1, DEV), F32)
    edges = []
    for kind in cls:
        ind = kind.astype(F32)
        before = jnp.dot(jnp.broadcast_to(ind, (8, DEV)).astype(BF16), upper, preferred_element_type=F32)[0:1]
        spot = spot + ind * (before + base)
        base = base + jnp.sum(ind, axis=1, keepdims=True)
        edges.append(base)
    here = (jnp.broadcast_to(spot, (DEV, DEV)) == row_i.astype(F32)).astype(BF16)
    names = lax.broadcasted_iota(I32, (8, DEV), 1).astype(F32).astype(BF16)
    list_ref[...] = lax.dot_general(
        names, here, (((1,), (1,)), ((), ())), preferred_element_type=F32
    ).astype(I32)
    edge_lane = lax.broadcasted_iota(I32, (8, DEV), 1)
    edge = jnp.where(edge_lane == 0, edges[0], jnp.where(edge_lane == 1, edges[1], edges[2]))
    edge_ref[...] = edge.astype(I32)


class Exchange:
    def __init__(self, axis, size, source, target, send, recv, peers=None, keep=True):
        self.axis, self.size, self.source, self.target = axis, size, source, target
        self.send, self.recv, self.keep = send, recv, keep
        self.me = lax.axis_index(axis)
        self.peers = peers if peers is not None else lambda k: lax.rem(self.me + k, size)

    def copy(self, k):
        peer = self.peers(k)
        return pltpu.make_async_remote_copy(
            src_ref=self.source(peer),
            dst_ref=self.target(self.me),
            send_sem=self.send.at[k],
            recv_sem=self.recv.at[k],
            device_id={self.axis: peer},
            device_id_type=pl.DeviceIdType.MESH,
        )

    def own(self):
        return pltpu.make_async_copy(self.source(self.me), self.target(self.me), self.recv.at[0])

    def start(self):
        def step(k, _):
            self.copy(k).start()
            return 0

        lax.fori_loop(1, self.size, step, 0)
        if self.keep:
            self.own().start()

    def wait_recv(self):
        def step(k, _):
            self.copy(k).wait_recv()
            return 0

        lax.fori_loop(1, self.size, step, 0)
        if self.keep:
            self.own().wait()

    def wait_send(self):
        def step(k, _):
            self.copy(k).wait_send()
            return 0

        lax.fori_loop(1, self.size, step, 0)


def greet(axes):
    barrier = pltpu.get_barrier_semaphore()
    for axis, size in axes:
        me = lax.axis_index(axis)

        def step(k, _, axis=axis, size=size, me=me):
            pl.semaphore_signal(
                barrier, inc=1, device_id={axis: lax.rem(me + k, size)}, device_id_type=pl.DeviceIdType.MESH
            )
            return 0

        lax.fori_loop(1, size, step, 0)


def spectrum_kernel(
    rcv_ref,
    src_ref,
    traces_ref,
    first_ref,
    second_ref,
    data_first_ref,
    data_second_ref,
    cell_rows_ref,
    count_ref,
    start_ref,
    list_ref,
    edge_ref,
    x_ref,
    table_ref,
    pick_ref,
    spec_ref,
    spread_ref,
    cell_send,
    cell_mid,
    cell_pack,
    cell_all,
    code_wide,
    first_send,
    first_mid,
    second_send,
    second_mid,
    load_sem,
    bin_send,
    bin_recv,
    freq_send,
    freq_recv,
    core_send,
    core_recv,
):
    def over_bin(slot, source, target):
        return Exchange("bin", 8, source, target, bin_send.at[slot], bin_recv.at[slot])

    def over_freq(slot, source, target):
        return Exchange("freq", 16, source, target, freq_send.at[slot], freq_recv.at[slot])

    bin_me = lax.axis_index("bin")
    core, x_me = lax.rem(bin_me, 2), bin_me // 2
    cell_freq = over_freq(0, lambda f: cell_send, lambda me: cell_mid.at[me])
    cell_x = Exchange(
        "bin",
        4,
        lambda b: cell_pack,
        lambda me: cell_all.at[core, x_me],
        bin_send.at[0],
        bin_recv.at[0],
        peers=lambda k: lax.rem(bin_me + 2 * k, 8),
    )
    cell_core = Exchange(
        "bin",
        2,
        lambda b: cell_all.at[core],
        lambda me: cell_all.at[core],
        core_send,
        core_recv,
        peers=lambda k: bin_me + 1 - 2 * core,
        keep=False,
    )
    first_bin = over_bin(1, lambda b: first_send.at[b], lambda me: first_mid.at[me])
    first_freq = over_freq(1, lambda f: first_mid.at[:, f], lambda me: data_first_ref.at[me])
    second_freq = over_freq(2, lambda f: second_send.at[f], lambda me: second_mid.at[me])
    second_bin = over_bin(2, lambda b: second_mid.at[:, b], lambda me: data_second_ref.at[me])

    def load_traces(m):
        at = pl.ds(m * 256, 256)
        return pltpu.make_async_copy(traces_ref.at[at], x_ref.at[at], load_sem.at[m])

    def load_table(h):
        return pltpu.make_async_copy((first_ref, second_ref)[h], table_ref.at[h], load_sem.at[4 + h])

    greet((("bin", 8), ("freq", 16)))
    load_table(0).start()
    for m in range(4):
        load_traces(m).start()
    load_table(1).start()
    carry, upper, row_i = index_work(rcv_ref, src_ref, pick_ref, cell_send, count_ref, start_ref)
    pl.semaphore_wait(pltpu.get_barrier_semaphore(), 22)
    cell_freq.start()
    list_runs(carry, upper, row_i, list_ref, edge_ref)

    def transform(h):
        load_table(h).wait()

        def rows(m, _):
            if h == 0:
                load_traces(m).wait()
            at = pl.ds(pl.multiple_of(m * 256, 256), 256)
            both = jnp.dot(x_ref[at, :], table_ref[h], preferred_element_type=F32)
            spec_ref[at, :] = (both[:, :256] + both[:, 256:]).astype(BF16)
            return 0

        lax.fori_loop(0, 4, rows, 0)

    def sort_rows():
        for half in range(2):
            q = half * 512
            rows = lax.dot_general(
                spec_ref[...], pick_ref[:, q : q + 512], (((0,), (0,)), ((), ())), preferred_element_type=F32
            )
            for blk in range(4):
                spread_ref[pl.ds(half * 4 + blk, 256, stride=8), :] = rows[:, blk * DEV : (blk + 1) * DEV]

    transform(0)
    cell_freq.wait_recv()
    cell_pack[...] = cell_mid[...].reshape(DEV, DEV).astype(jnp.int16)
    cell_x.start()
    sort_rows()
    for b in range(8):
        first_send[b] = spread_ref[b * 256 : (b + 1) * 256, :].reshape(16, 16, DEV).astype(BF16)
    first_bin.start()
    transform(1)
    cell_x.wait_recv()
    cell_core.start()
    sort_rows()
    for f in range(16):
        second_send[f] = spread_ref[f * 128 : (f + 1) * 128, :].reshape(8, 16, DEV).astype(BF16)
    second_freq.start()
    first_bin.wait_recv()
    first_freq.start()
    cell_core.wait_recv()
    for c in range(2):
        for x in range(4):
            at = (x * 2 + c) * DEV
            code_wide[at : at + DEV, :] = cell_all[c, x].astype(F32)
    stride = TR + 16
    for blk in range(8):
        code = code_wide[pl.ds(blk, DEV, stride=8), :].T.astype(I32)
        cell_rows_ref[blk * DEV : (blk + 1) * DEV, :] = (code >> 6).astype(F32)
        cell_rows_ref[stride + blk * DEV : stride + (blk + 1) * DEV, :] = (code & 63).astype(F32)
    for digit in range(2):
        cell_rows_ref[digit * stride + TR : (digit + 1) * stride, :] = jnp.zeros((16, DEV), F32)
    second_freq.wait_recv()
    second_bin.start()
    first_freq.wait_recv()
    second_bin.wait_recv()
    for part in (cell_freq, cell_x, cell_core, first_bin, first_freq, second_freq, second_bin):
        part.wait_send()


def layout_kernel(
    count_ref,
    start_ref,
    list_ref,
    edge_ref,
    first_ref,
    second_ref,
    cell_ref,
    dense_ref,
    first_wide,
    second_wide,
    rows_ref,
    raw_ref,
):
    stride = TR + 16
    for b in range(8):
        second_wide[b * 256 : (b + 1) * 256, :] = second_ref[b].reshape(256, DEV).astype(F32)
        for f in range(16):
            at = (b * 16 + f) * 16
            first_wide[at : at + 16, :] = first_ref[f, b].astype(F32)
    for blk in range(8):
        for part in range(2):
            pick = pl.ds(part * 8 + blk, DEV, stride=16)
            rows_ref[pl.ds(part * stride + blk * DEV, DEV), :] = first_wide[pick, :].T
            rows_ref[pl.ds((2 + part) * stride + blk * DEV, DEV), :] = second_wide[pick, :].T
    pad = jnp.zeros((16, DEV), F32)
    for comp in range(4):
        rows_ref[pl.ds(comp * stride + TR, 16), :] = pad

    sub32 = lax.broadcasted_iota(I32, (32, DEV), 0).astype(F32)
    sub64 = lax.broadcasted_iota(I32, (64, DEV), 0).astype(F32).astype(BF16)
    one, zero = jnp.ones((), BF16), jnp.zeros((), BF16)

    def lay_out(run, size):
        count = count_ref[0, run]
        start = start_ref[0, run]
        left, right = [], []
        for j in range(size):
            at = start + j
            high = jnp.broadcast_to(cell_ref[pl.ds(at, 1), :], (32, DEV))
            hit = jnp.where(j < count, high, -1.0) == sub32
            parts = []
            for comp in range(4):
                row = jnp.broadcast_to(rows_ref[pl.ds(comp * stride + at, 1), :], (32, DEV))
                parts.append(jnp.where(hit, row, 0.0).astype(BF16))
            left.append(jnp.concatenate(parts, axis=0))
            low = jnp.broadcast_to(cell_ref[pl.ds(stride + at, 1), :], (16, DEV)).astype(BF16)
            right.append(jnp.where(jnp.concatenate([low] * 4, axis=0) == sub64, one, zero))
        raw_ref[run, :, 0:64] = lax.dot_general(
            jnp.concatenate(left, axis=1),
            jnp.concatenate(right, axis=1),
            (((1,), (1,)), ((), ())),
            preferred_element_type=F32,
        )

    begin = 0
    for kind, (size, together) in enumerate(((4, 8), (8, 8), (16, 4))):
        end = edge_ref[0, kind]

        def some_runs(step, _, begin=begin, end=end, size=size, together=together):
            for u in range(together):
                lay_out(list_ref[0, jnp.minimum(begin + step * together + u, end - 1)], size)
            return 0

        lax.fori_loop(0, (end - begin + together - 1) // together, some_runs, 0)
        begin = end

    top = lax.broadcasted_iota(I32, (8, DEV), 0) < 4
    left_half = lax.broadcasted_iota(I32, (8, DEV), 1) < 64

    def four_runs(group, _):
        for comp in range(4):
            at = pl.ds(pl.multiple_of(comp * ORDER + group * 16, 16), 16)
            for tile in range(4):
                sl = pl.ds(comp * 32 + 8 * tile, 8)
                merged = []
                for pair in range(2):
                    even = raw_ref[4 * group + 2 * pair, sl, :]
                    odd = raw_ref[4 * group + 2 * pair + 1, sl, :]
                    right = pltpu.roll(pltpu.roll(jnp.where(top, odd, even), 4, 0), 64, 1)
                    merged.append(jnp.where(left_half, jnp.where(top, even, odd), right))
                dense_ref[at, pl.ds(tile * DEV, DEV)] = jnp.concatenate(merged, axis=0).astype(BF16)
        return 0

    lax.fori_loop(0, DEV // 4, four_runs, 0, unroll=2)


def product_kernel(filt_ref, dense_ref, out_ref, block_ref, send, recv):
    mine = lax.axis_index("bin") * 2
    amplitude = 1.0 / math.sqrt(ORDER)
    greet((("bin", 8),))
    moves = [
        Exchange(
            "bin",
            8,
            lambda b, i=i: block_ref.at[b, i],
            lambda me, i=i: out_ref.at[:, me * 2 + i],
            send.at[i],
            recv.at[i],
        )
        for i in range(2)
    ]
    for i in range(2):
        real = dense_ref[pl.ds(2 * i * ORDER, ORDER), :]
        imag = dense_ref[pl.ds((2 * i + 1) * ORDER, ORDER), :]
        fr = filt_ref[0, mine + i]
        fi = filt_ref[1, mine + i]
        for t in range(2):
            cols = slice(t * 256, (t + 1) * 256)
            rc, ic = real[:, cols], imag[:, cols]
            dot = functools.partial(jnp.dot, preferred_element_type=F32)
            sr = dot(real, rc) - dot(imag, ic)
            si = dot(real, ic) + dot(imag, rc)
            outr = ((fr * sr - fi * si) * amplitude).astype(BF16)
            outi = ((fr * si + fi * sr) * amplitude).astype(BF16)
            for b in range(8):
                block_ref[b, i, 0, :, cols] = outr[b * 64 : (b + 1) * 64]
                block_ref[b, i, 1, :, cols] = outi[b * 64 : (b + 1) * 64]
        if i == 0:
            pl.semaphore_wait(pltpu.get_barrier_semaphore(), 7)
        moves[i].start()
    for move in moves:
        move.wait_recv()
        move.wait_send()


def local(traces, rcv_index, src_index, wave_filter):
    tables = dft_tables()
    params = pltpu.CompilerParams(vmem_limit_bytes=LIMIT)
    vmem = pl.BlockSpec(memory_space=pltpu.VMEM)
    smem = pl.BlockSpec(memory_space=pltpu.SMEM)
    anywhere = pl.BlockSpec(memory_space=pl.ANY)
    shape = jax.ShapeDtypeStruct
    small = shape((8, DEV), I32)
    dma = pltpu.SemaphoreType.DMA
    outgoing, middle = pltpu.VMEM((8, 16, 16, DEV), BF16), pltpu.VMEM((16, 8, 16, DEV), BF16)
    first, second, cells, count, start, listed, edge = pl.pallas_call(
        spectrum_kernel,
        in_specs=[vmem, vmem, anywhere, anywhere, anywhere],
        out_specs=(anywhere, anywhere, vmem, vmem, vmem, vmem, vmem),
        out_shape=(
            shape((16, 8, 16, DEV), BF16),
            shape((8, 16, 16, DEV), BF16),
            shape((2 * (TR + 16), DEV), F32),
            small,
            small,
            small,
            small,
        ),
        scratch_shapes=[
            pltpu.VMEM((TR, NT), BF16),
            pltpu.VMEM((2, NT, 4 * DEV), BF16),
            pltpu.VMEM((TR, TR), BF16),
            pltpu.VMEM((TR, 256), BF16),
            pltpu.VMEM((2048, DEV), F32),
            pltpu.VMEM((8, DEV), I32),
            pltpu.VMEM((16, 8, DEV), I32),
            pltpu.VMEM((DEV, DEV), jnp.int16),
            pltpu.VMEM((2, 4, DEV, DEV), jnp.int16),
            pltpu.VMEM((TR, DEV), F32),
            outgoing,
            outgoing,
            middle,
            middle,
            dma((6,)),
            dma((3, 8)),
            dma((3, 8)),
            dma((3, 16)),
            dma((3, 16)),
            dma((2,)),
            dma((2,)),
        ],
        compiler_params=pltpu.CompilerParams(vmem_limit_bytes=LIMIT, collective_id=1, has_side_effects=True),
        cost_estimate=pl.CostEstimate(flops=5 * 10**9, bytes_accessed=9 * 10**6, transcendentals=0),
        name="spectrum",
    )(rcv_index.reshape(8, DEV), src_index.reshape(8, DEV), traces, jnp.asarray(tables[0]), jnp.asarray(tables[1]))
    dense = pl.pallas_call(
        layout_kernel,
        in_specs=[smem, smem, smem, smem, vmem, vmem, vmem],
        out_specs=vmem,
        out_shape=shape((4 * ORDER, ORDER), BF16),
        scratch_shapes=[
            pltpu.VMEM((2048, DEV), F32),
            pltpu.VMEM((2048, DEV), F32),
            pltpu.VMEM((4 * (TR + 16), DEV), F32),
            pltpu.VMEM((DEV, DEV, DEV), F32),
        ],
        compiler_params=params,
        name="layout",
    )(count, start, listed, edge, first, second, cells)
    return pl.pallas_call(
        product_kernel,
        in_specs=[smem, vmem],
        out_specs=anywhere,
        out_shape=shape((2, 16, 64, ORDER), BF16),
        scratch_shapes=[pltpu.VMEM((8, 2, 2, 64, ORDER), BF16), dma((2, 8)), dma((2, 8))],
        compiler_params=pltpu.CompilerParams(vmem_limit_bytes=LIMIT, collective_id=2, has_side_effects=True),
        name="product",
    )(wave_filter, dense)


def solution(mesh):
    placed = (P(("bin", "freq"), None), P(("bin", "freq")), P(("bin", "freq")), P(None, "freq"))
    return jax.shard_map(
        local, mesh=mesh, in_specs=placed, out_specs=P(None, "freq", "bin", None), check_vma=False
    )
```

```python
import functools
import math

import jax
import jax.numpy as jnp
import numpy as np
from jax import lax
from jax.experimental import pallas as pl
from jax.experimental.pallas import tpu as pltpu
from jax.sharding import PartitionSpec as P
import ml_dtypes

ORDER = 512
NT = 2048
NF = 256
DEV = 128
TR = 1024
F32 = jnp.float32
BF16 = jnp.bfloat16
I32 = jnp.int32
LIMIT = 56 * 1024 * 1024


def dft_tables():
    bins, freqs, part = np.meshgrid(np.arange(8), np.arange(16), np.arange(2), indexing="ij")
    first = freqs * 16 + bins * 2
    order = (1, 0, 2)
    freq = np.concatenate([first.reshape(-1), (first + 1).transpose(order).reshape(-1)])
    part = np.concatenate([part.reshape(-1), part.transpose(order).reshape(-1)])
    phase = (np.arange(NT)[:, None] * freq[None, :]) % NT
    angle = 2.0 * np.pi / NT * phase
    table = np.where(part[None, :] == 0, np.cos(angle), -np.sin(angle)) / math.sqrt(NT)
    high = table.astype(ml_dtypes.bfloat16)
    low = (table - high.astype(np.float64)).astype(ml_dtypes.bfloat16)
    return [np.concatenate([high[:, h : h + 256], low[:, h : h + 256]], axis=1) for h in (0, 256)]


def index_work(rcv_ref, src_ref, pick_ref, cell_ref, count_ref, start_ref):
    lane = lax.broadcasted_iota(I32, (TR, DEV), 1)
    row_i = lax.broadcasted_iota(I32, (DEV, DEV), 0)
    col_i = lax.broadcasted_iota(I32, (DEV, DEV), 1)
    lower = (col_i < row_i).astype(BF16)
    upper = (row_i < col_i).astype(BF16)
    same = row_i == col_i
    rcv = rcv_ref[...]
    src = src_ref[...]
    run = (rcv >> 2).astype(F32)
    columns = []
    for blk in range(TR // DEV):
        spread = jnp.where(same, jnp.broadcast_to(run[blk : blk + 1, :], (DEV, DEV)), 0.0)
        columns.append(jnp.sum(spread, axis=1, keepdims=True))
    member = (jnp.concatenate(columns, axis=0).astype(I32) == lane).astype(F32)
    carry = jnp.zeros((1, DEV), F32)
    ranks = []
    for blk in range(TR // DEV):
        m = member[blk * DEV : (blk + 1) * DEV]
        ranks.append(jnp.dot(lower, m.astype(BF16), preferred_element_type=F32) + carry)
        carry = carry + jnp.sum(m, axis=0, keepdims=True)
    rank_all = jnp.concatenate(ranks, axis=0)
    counts8 = jnp.broadcast_to(carry, (8, DEV))
    start = jnp.dot(counts8.astype(BF16), upper, preferred_element_type=F32)
    place = jnp.sum(member * (rank_all + start[0:1]), axis=1, keepdims=True).astype(I32)
    count_ref[...] = counts8.astype(I32)
    start_ref[...] = start.astype(I32)
    pick_ref[...] = (place == lax.broadcasted_iota(I32, (TR, TR), 1)).astype(F32).astype(BF16)
    half = ((src >> 6) + (rcv >> 2)) & 1
    high = ((src >> 7) * 8 + half * 4 + (rcv & 3)).astype(F32)
    low = (src & 63).astype(F32)
    flat = [jnp.concatenate([v[blk : blk + 1, :] for blk in range(TR // DEV)], axis=1) for v in (high, low)]
    digits = jnp.concatenate([jnp.broadcast_to(v, (8, TR)) for v in flat], axis=0).astype(BF16)
    both = jnp.dot(digits, pick_ref[...], preferred_element_type=F32)
    for blk in range(TR // DEV):
        cols = slice(blk * DEV, (blk + 1) * DEV)
        cell_ref[blk : blk + 1, :] = (both[0:1, cols] * 64.0 + both[8:9, cols]).astype(I32)
    return carry, upper, row_i


def list_runs(carry, upper, row_i, list_ref, edge_ref):
    cls = [carry <= 4.0, (carry > 4.0) & (carry <= 8.0), carry > 8.0]
    base = jnp.zeros((1, 1), F32)
    spot = jnp.zeros((1, DEV), F32)
    edges = []
    for kind in cls:
        ind = kind.astype(F32)
        before = jnp.dot(jnp.broadcast_to(ind, (8, DEV)).astype(BF16), upper, preferred_element_type=F32)[0:1]
        spot = spot + ind * (before + base)
        base = base + jnp.sum(ind, axis=1, keepdims=True)
        edges.append(base)
    here = (jnp.broadcast_to(spot, (DEV, DEV)) == row_i.astype(F32)).astype(BF16)
    names = lax.broadcasted_iota(I32, (8, DEV), 1).astype(F32).astype(BF16)
    list_ref[...] = lax.dot_general(
        names, here, (((1,), (1,)), ((), ())), preferred_element_type=F32
    ).astype(I32)
    edge_lane = lax.broadcasted_iota(I32, (8, DEV), 1)
    edge = jnp.where(edge_lane == 0, edges[0], jnp.where(edge_lane == 1, edges[1], edges[2]))
    edge_ref[...] = edge.astype(I32)


class Exchange:
    def __init__(self, axis, size, source, target, send, recv, peers=None, keep=True):
        self.axis, self.size, self.source, self.target = axis, size, source, target
        self.send, self.recv, self.keep = send, recv, keep
        self.me = lax.axis_index(axis)
        self.peers = peers if peers is not None else lambda k: lax.rem(self.me + k, size)

    def copy(self, k):
        peer = self.peers(k)
        return pltpu.make_async_remote_copy(
            src_ref=self.source(peer),
            dst_ref=self.target(self.me),
            send_sem=self.send.at[k],
            recv_sem=self.recv.at[k],
            device_id={self.axis: peer},
            device_id_type=pl.DeviceIdType.MESH,
        )

    def own(self):
        return pltpu.make_async_copy(self.source(self.me), self.target(self.me), self.recv.at[0])

    def start(self):
        def step(k, _):
            self.copy(k).start()
            return 0

        lax.fori_loop(1, self.size, step, 0)
        if self.keep:
            self.own().start()

    def wait_recv(self):
        def step(k, _):
            self.copy(k).wait_recv()
            return 0

        lax.fori_loop(1, self.size, step, 0)
        if self.keep:
            self.own().wait()

    def wait_send(self):
        def step(k, _):
            self.copy(k).wait_send()
            return 0

        lax.fori_loop(1, self.size, step, 0)


def greet(axes):
    barrier = pltpu.get_barrier_semaphore()
    for axis, size in axes:
        me = lax.axis_index(axis)

        def step(k, _, axis=axis, size=size, me=me):
            pl.semaphore_signal(
                barrier, inc=1, device_id={axis: lax.rem(me + k, size)}, device_id_type=pl.DeviceIdType.MESH
            )
            return 0

        lax.fori_loop(1, size, step, 0)


def spectrum_kernel(
    rcv_ref,
    src_ref,
    traces_ref,
    first_ref,
    second_ref,
    data_first_ref,
    data_second_ref,
    cell_rows_ref,
    count_ref,
    start_ref,
    list_ref,
    edge_ref,
    x_ref,
    table_ref,
    pick_ref,
    spec_ref,
    spread_ref,
    cell_send,
    cell_mid,
    cell_pack,
    cell_all,
    code_wide,
    first_send,
    first_mid,
    second_send,
    second_mid,
    load_sem,
    bin_send,
    bin_recv,
    freq_send,
    freq_recv,
    core_send,
    core_recv,
):
    def over_bin(slot, source, target):
        return Exchange("bin", 8, source, target, bin_send.at[slot], bin_recv.at[slot])

    def over_freq(slot, source, target):
        return Exchange("freq", 16, source, target, freq_send.at[slot], freq_recv.at[slot])

    bin_me = lax.axis_index("bin")
    core, x_me = lax.rem(bin_me, 2), bin_me // 2
    cell_freq = over_freq(0, lambda f: cell_send, lambda me: cell_mid.at[me])
    cell_x = Exchange(
        "bin",
        4,
        lambda b: cell_pack,
        lambda me: cell_all.at[core, x_me],
        bin_send.at[0],
        bin_recv.at[0],
        peers=lambda k: lax.rem(bin_me + 2 * k, 8),
    )
    cell_core = Exchange(
        "bin",
        2,
        lambda b: cell_all.at[core],
        lambda me: cell_all.at[core],
        core_send,
        core_recv,
        peers=lambda k: bin_me + 1 - 2 * core,
        keep=False,
    )
    first_bin = over_bin(1, lambda b: first_send.at[b], lambda me: first_mid.at[me])
    first_freq = over_freq(1, lambda f: first_mid.at[:, f], lambda me: data_first_ref.at[me])
    second_freq = over_freq(2, lambda f: second_send.at[f], lambda me: second_mid.at[me])
    second_bin = over_bin(2, lambda b: second_mid.at[:, b], lambda me: data_second_ref.at[me])

    def load_traces(m):
        at = pl.ds(m * 256, 256)
        return pltpu.make_async_copy(traces_ref.at[at], x_ref.at[at], load_sem.at[m])

    def load_table(h):
        return pltpu.make_async_copy((first_ref, second_ref)[h], table_ref.at[h], load_sem.at[4 + h])

    greet((("bin", 8), ("freq", 16)))
    load_table(0).start()
    for m in range(4):
        load_traces(m).start()
    load_table(1).start()
    carry, upper, row_i = index_work(rcv_ref, src_ref, pick_ref, cell_send, count_ref, start_ref)
    pl.semaphore_wait(pltpu.get_barrier_semaphore(), 22)
    cell_freq.start()
    list_runs(carry, upper, row_i, list_ref, edge_ref)

    def transform(h):
        load_table(h).wait()

        def rows(m, _):
            if h == 0:
                load_traces(m).wait()
            at = pl.ds(pl.multiple_of(m * 256, 256), 256)
            both = jnp.dot(x_ref[at, :], table_ref[h], preferred_element_type=F32)
            spec_ref[at, :] = (both[:, :256] + both[:, 256:]).astype(BF16)
            return 0

        lax.fori_loop(0, 4, rows, 0)

    def sort_rows():
        for half in range(2):
            q = half * 512
            rows = lax.dot_general(
                spec_ref[...], pick_ref[:, q : q + 512], (((0,), (0,)), ((), ())), preferred_element_type=F32
            )
            for blk in range(4):
                spread_ref[pl.ds(half * 4 + blk, 256, stride=8), :] = rows[:, blk * DEV : (blk + 1) * DEV]

    transform(0)
    cell_freq.wait_recv()
    cell_pack[...] = cell_mid[...].reshape(DEV, DEV).astype(jnp.int16)
    cell_x.start()
    sort_rows()
    for b in range(8):
        first_send[b] = spread_ref[b * 256 : (b + 1) * 256, :].reshape(16, 16, DEV).astype(BF16)
    first_bin.start()
    transform(1)
    sort_rows()
    for f in range(16):
        second_send[f] = spread_ref[f * 128 : (f + 1) * 128, :].reshape(8, 16, DEV).astype(BF16)
    second_freq.start()
    first_bin.wait_recv()
    first_freq.start()
    cell_x.wait_recv()
    cell_core.start()
    cell_core.wait_recv()
    for c in range(2):
        for x in range(4):
            at = (x * 2 + c) * DEV
            code_wide[at : at + DEV, :] = cell_all[c, x].astype(F32)
    stride = TR + 16
    for blk in range(8):
        code = code_wide[pl.ds(blk, DEV, stride=8), :].T.astype(I32)
        cell_rows_ref[blk * DEV : (blk + 1) * DEV, :] = (code >> 6).astype(F32)
        cell_rows_ref[stride + blk * DEV : stride + (blk + 1) * DEV, :] = (code & 63).astype(F32)
    for digit in range(2):
        cell_rows_ref[digit * stride + TR : (digit + 1) * stride, :] = jnp.zeros((16, DEV), F32)
    second_freq.wait_recv()
    second_bin.start()
    first_freq.wait_recv()
    second_bin.wait_recv()
    for part in (cell_freq, cell_x, cell_core, first_bin, first_freq, second_freq, second_bin):
        part.wait_send()


def layout_kernel(
    count_ref,
    start_ref,
    list_ref,
    edge_ref,
    first_ref,
    second_ref,
    cell_ref,
    dense_ref,
    first_wide,
    second_wide,
    rows_ref,
    raw_ref,
):
    stride = TR + 16
    for b in range(8):
        second_wide[b * 256 : (b + 1) * 256, :] = second_ref[b].reshape(256, DEV).astype(F32)
        for f in range(16):
            at = (b * 16 + f) * 16
            first_wide[at : at + 16, :] = first_ref[f, b].astype(F32)
    for blk in range(8):
        for part in range(2):
            pick = pl.ds(part * 8 + blk, DEV, stride=16)
            rows_ref[pl.ds(part * stride + blk * DEV, DEV), :] = first_wide[pick, :].T
            rows_ref[pl.ds((2 + part) * stride + blk * DEV, DEV), :] = second_wide[pick, :].T
    pad = jnp.zeros((16, DEV), F32)
    for comp in range(4):
        rows_ref[pl.ds(comp * stride + TR, 16), :] = pad

    sub32 = lax.broadcasted_iota(I32, (32, DEV), 0).astype(F32).astype(BF16)
    sub64 = lax.broadcasted_iota(I32, (64, DEV), 0).astype(F32).astype(BF16)
    one, zero = jnp.ones((), BF16), jnp.zeros((), BF16)

    def lay_out(run, size):
        count = count_ref[0, run]
        start = start_ref[0, run]
        left, right = [], []
        for j in range(size):
            at = start + j
            high = jnp.broadcast_to(cell_ref[pl.ds(at, 1), :], (16, DEV))
            high = jnp.where(j < count, high, -1.0).astype(BF16)
            hit = jnp.concatenate([high] * 2, axis=0) == sub32
            parts = []
            for comp in range(4):
                row = jnp.broadcast_to(rows_ref[pl.ds(comp * stride + at, 1), :], (16, DEV)).astype(BF16)
                parts.append(jnp.where(hit, jnp.concatenate([row] * 2, axis=0), zero))
            left.append(jnp.concatenate(parts, axis=0))
            low = jnp.broadcast_to(cell_ref[pl.ds(stride + at, 1), :], (16, DEV)).astype(BF16)
            right.append(jnp.where(jnp.concatenate([low] * 4, axis=0) == sub64, one, zero))
        raw_ref[run, :, 0:64] = lax.dot_general(
            jnp.concatenate(left, axis=1),
            jnp.concatenate(right, axis=1),
            (((1,), (1,)), ((), ())),
            preferred_element_type=F32,
        )

    begin = 0
    for kind, (size, together) in enumerate(((4, 32), (8, 32), (16, 16))):
        end = edge_ref[0, kind]

        def some_runs(step, _, begin=begin, end=end, size=size, together=together):
            for u in range(together):
                lay_out(list_ref[0, jnp.minimum(begin + step * together + u, end - 1)], size)
            return 0

        lax.fori_loop(0, (end - begin + together - 1) // together, some_runs, 0)
        begin = end

    top = lax.broadcasted_iota(I32, (8, DEV), 0) < 4
    left_half = lax.broadcasted_iota(I32, (8, DEV), 1) < 64

    def four_runs(group, _):
        for comp in range(4):
            at = pl.ds(pl.multiple_of(comp * ORDER + group * 16, 16), 16)
            for tile in range(4):
                sl = pl.ds(comp * 32 + 8 * tile, 8)
                merged = []
                for pair in range(2):
                    even = raw_ref[4 * group + 2 * pair, sl, :]
                    odd = raw_ref[4 * group + 2 * pair + 1, sl, :]
                    right = pltpu.roll(pltpu.roll(jnp.where(top, odd, even), 4, 0), 64, 1)
                    merged.append(jnp.where(left_half, jnp.where(top, even, odd), right))
                dense_ref[at, pl.ds(tile * DEV, DEV)] = jnp.concatenate(merged, axis=0).astype(BF16)
        return 0

    lax.fori_loop(0, DEV // 4, four_runs, 0, unroll=2)


def product_kernel(filt_ref, dense_ref, out_ref, block_ref, send, recv):
    mine = lax.axis_index("bin") * 2
    amplitude = 1.0 / math.sqrt(ORDER)
    greet((("bin", 8),))
    moves = [
        Exchange(
            "bin",
            8,
            lambda b, i=i: block_ref.at[b, i],
            lambda me, i=i: out_ref.at[:, me * 2 + i],
            send.at[i],
            recv.at[i],
        )
        for i in range(2)
    ]
    for i in range(2):
        real = dense_ref[pl.ds(2 * i * ORDER, ORDER), :]
        imag = dense_ref[pl.ds((2 * i + 1) * ORDER, ORDER), :]
        fr = filt_ref[0, mine + i]
        fi = filt_ref[1, mine + i]
        for t in range(2):
            cols = slice(t * 256, (t + 1) * 256)
            rc, ic = real[:, cols], imag[:, cols]
            dot = functools.partial(jnp.dot, preferred_element_type=F32)
            sr = dot(real, rc) - dot(imag, ic)
            si = dot(real, ic) + dot(imag, rc)
            outr = ((fr * sr - fi * si) * amplitude).astype(BF16)
            outi = ((fr * si + fi * sr) * amplitude).astype(BF16)
            for b in range(8):
                block_ref[b, i, 0, :, cols] = outr[b * 64 : (b + 1) * 64]
                block_ref[b, i, 1, :, cols] = outi[b * 64 : (b + 1) * 64]
        if i == 0:
            pl.semaphore_wait(pltpu.get_barrier_semaphore(), 7)
        moves[i].start()
    for move in moves:
        move.wait_recv()
        move.wait_send()


def hand_over(rows_ref, out_ref, hold_ref, sem):
    loads = [pltpu.make_async_copy(rows_ref.at[:, i], hold_ref.at[:, i], sem.at[0, i]) for i in range(16)]
    stores = [pltpu.make_async_copy(hold_ref.at[:, i], out_ref.at[:, i], sem.at[1, i]) for i in range(16)]
    for load in loads:
        load.start()
    for load, store in zip(loads, stores):
        load.wait()
        store.start()
    for store in stores:
        store.wait()


def local(traces, rcv_index, src_index, wave_filter):
    tables = dft_tables()
    params = pltpu.CompilerParams(vmem_limit_bytes=LIMIT)
    vmem = pl.BlockSpec(memory_space=pltpu.VMEM)
    smem = pl.BlockSpec(memory_space=pltpu.SMEM)
    anywhere = pl.BlockSpec(memory_space=pl.ANY)
    shape = jax.ShapeDtypeStruct
    small = shape((8, DEV), I32)
    dma = pltpu.SemaphoreType.DMA
    outgoing, middle = pltpu.VMEM((8, 16, 16, DEV), BF16), pltpu.VMEM((16, 8, 16, DEV), BF16)
    first, second, cells, count, start, listed, edge = pl.pallas_call(
        spectrum_kernel,
        in_specs=[vmem, vmem, anywhere, anywhere, anywhere],
        out_specs=(anywhere, anywhere, vmem, vmem, vmem, vmem, vmem),
        out_shape=(
            shape((16, 8, 16, DEV), BF16),
            shape((8, 16, 16, DEV), BF16),
            shape((2 * (TR + 16), DEV), F32),
            small,
            small,
            small,
            small,
        ),
        scratch_shapes=[
            pltpu.VMEM((TR, NT), BF16),
            pltpu.VMEM((2, NT, 4 * DEV), BF16),
            pltpu.VMEM((TR, TR), BF16),
            pltpu.VMEM((TR, 256), BF16),
            pltpu.VMEM((2048, DEV), F32),
            pltpu.VMEM((8, DEV), I32),
            pltpu.VMEM((16, 8, DEV), I32),
            pltpu.VMEM((DEV, DEV), jnp.int16),
            pltpu.VMEM((2, 4, DEV, DEV), jnp.int16),
            pltpu.VMEM((TR, DEV), F32),
            outgoing,
            outgoing,
            middle,
            middle,
            dma((6,)),
            dma((3, 8)),
            dma((3, 8)),
            dma((3, 16)),
            dma((3, 16)),
            dma((2,)),
            dma((2,)),
        ],
        compiler_params=pltpu.CompilerParams(vmem_limit_bytes=LIMIT, collective_id=1, has_side_effects=True),
        cost_estimate=pl.CostEstimate(flops=5 * 10**9, bytes_accessed=9 * 10**6, transcendentals=0),
        name="spectrum",
    )(rcv_index.reshape(8, DEV), src_index.reshape(8, DEV), traces, jnp.asarray(tables[0]), jnp.asarray(tables[1]))
    dense = pl.pallas_call(
        layout_kernel,
        in_specs=[smem, smem, smem, smem, vmem, vmem, vmem],
        out_specs=vmem,
        out_shape=shape((4 * ORDER, ORDER), BF16),
        scratch_shapes=[
            pltpu.VMEM((2048, DEV), F32),
            pltpu.VMEM((2048, DEV), F32),
            pltpu.VMEM((4 * (TR + 16), DEV), F32),
            pltpu.VMEM((DEV, DEV, DEV), F32),
        ],
        compiler_params=params,
        name="layout",
    )(count, start, listed, edge, first, second, cells)
    rows = pl.pallas_call(
        product_kernel,
        in_specs=[smem, vmem],
        out_specs=anywhere,
        out_shape=shape((2, 16, 64, ORDER), BF16),
        scratch_shapes=[pltpu.VMEM((8, 2, 2, 64, ORDER), BF16), dma((2, 8)), dma((2, 8))],
        compiler_params=pltpu.CompilerParams(vmem_limit_bytes=LIMIT, collective_id=2, has_side_effects=True),
        name="product",
    )(wave_filter, dense)
    return pl.pallas_call(
        hand_over,
        in_specs=[anywhere],
        out_specs=anywhere,
        out_shape=shape((2, 16, 64, ORDER), BF16),
        scratch_shapes=[pltpu.VMEM((2, 16, 64, ORDER), BF16), dma((2, 16))],
        compiler_params=params,
        name="hand_over",
    )(rows)


def solution(mesh):
    placed = (P(("bin", "freq"), None), P(("bin", "freq")), P(("bin", "freq")), P(None, "freq"))
    return jax.shard_map(
        local, mesh=mesh, in_specs=placed, out_specs=P(None, "freq", "bin", None), check_vma=False
    )
```

```python
import functools
import math

import jax
import jax.numpy as jnp
import numpy as np
from jax import lax
from jax.experimental import pallas as pl
from jax.experimental.pallas import tpu as pltpu
from jax.sharding import PartitionSpec as P
import ml_dtypes

ORDER = 512
NT = 2048
NF = 256
DEV = 128
TR = 1024
F32 = jnp.float32
BF16 = jnp.bfloat16
I32 = jnp.int32
LIMIT = 56 * 1024 * 1024


def dft_tables():
    bins, freqs, part = np.meshgrid(np.arange(8), np.arange(16), np.arange(2), indexing="ij")
    first = freqs * 16 + bins * 2
    order = (1, 0, 2)
    freq = np.concatenate([first.reshape(-1), (first + 1).transpose(order).reshape(-1)])
    part = np.concatenate([part.reshape(-1), part.transpose(order).reshape(-1)])
    phase = (np.arange(NT)[:, None] * freq[None, :]) % NT
    angle = 2.0 * np.pi / NT * phase
    table = np.where(part[None, :] == 0, np.cos(angle), -np.sin(angle)) / math.sqrt(NT)
    high = table.astype(ml_dtypes.bfloat16)
    low = (table - high.astype(np.float64)).astype(ml_dtypes.bfloat16)
    return [np.concatenate([high[:, h : h + 256], low[:, h : h + 256]], axis=1) for h in (0, 256)]


def index_work(rcv_ref, src_ref, pick_ref, cell_ref, count_ref, start_ref):
    lane = lax.broadcasted_iota(I32, (TR, DEV), 1)
    row_i = lax.broadcasted_iota(I32, (DEV, DEV), 0)
    col_i = lax.broadcasted_iota(I32, (DEV, DEV), 1)
    lower = (col_i < row_i).astype(BF16)
    upper = (row_i < col_i).astype(BF16)
    same = row_i == col_i
    rcv = rcv_ref[...]
    src = src_ref[...]
    run = (rcv >> 2).astype(F32)
    columns = []
    for blk in range(TR // DEV):
        spread = jnp.where(same, jnp.broadcast_to(run[blk : blk + 1, :], (DEV, DEV)), 0.0)
        columns.append(jnp.sum(spread, axis=1, keepdims=True))
    member = (jnp.concatenate(columns, axis=0).astype(I32) == lane).astype(F32)
    carry = jnp.zeros((1, DEV), F32)
    ranks = []
    for blk in range(TR // DEV):
        m = member[blk * DEV : (blk + 1) * DEV]
        ranks.append(jnp.dot(lower, m.astype(BF16), preferred_element_type=F32) + carry)
        carry = carry + jnp.sum(m, axis=0, keepdims=True)
    rank_all = jnp.concatenate(ranks, axis=0)
    counts8 = jnp.broadcast_to(carry, (8, DEV))
    start = jnp.dot(counts8.astype(BF16), upper, preferred_element_type=F32)
    place = jnp.sum(member * (rank_all + start[0:1]), axis=1, keepdims=True).astype(I32)
    count_ref[...] = counts8.astype(I32)
    start_ref[...] = start.astype(I32)
    pick_ref[...] = (place == lax.broadcasted_iota(I32, (TR, TR), 1)).astype(F32).astype(BF16)
    half = ((src >> 6) + (rcv >> 2)) & 1
    high = ((src >> 7) * 8 + half * 4 + (rcv & 3)).astype(F32)
    low = (src & 63).astype(F32)
    flat = [jnp.concatenate([v[blk : blk + 1, :] for blk in range(TR // DEV)], axis=1) for v in (high, low)]
    digits = jnp.concatenate([jnp.broadcast_to(v, (8, TR)) for v in flat], axis=0).astype(BF16)
    both = jnp.dot(digits, pick_ref[...], preferred_element_type=F32)
    for blk in range(TR // DEV):
        cols = slice(blk * DEV, (blk + 1) * DEV)
        cell_ref[blk : blk + 1, :] = (both[0:1, cols] * 64.0 + both[8:9, cols]).astype(I32)
    return carry, upper, row_i


def list_runs(carry, upper, row_i, list_ref, edge_ref):
    cls = [carry <= 4.0, (carry > 4.0) & (carry <= 8.0), carry > 8.0]
    base = jnp.zeros((1, 1), F32)
    spot = jnp.zeros((1, DEV), F32)
    edges = []
    for kind in cls:
        ind = kind.astype(F32)
        before = jnp.dot(jnp.broadcast_to(ind, (8, DEV)).astype(BF16), upper, preferred_element_type=F32)[0:1]
        spot = spot + ind * (before + base)
        base = base + jnp.sum(ind, axis=1, keepdims=True)
        edges.append(base)
    here = (jnp.broadcast_to(spot, (DEV, DEV)) == row_i.astype(F32)).astype(BF16)
    names = lax.broadcasted_iota(I32, (8, DEV), 1).astype(F32).astype(BF16)
    list_ref[...] = lax.dot_general(
        names, here, (((1,), (1,)), ((), ())), preferred_element_type=F32
    ).astype(I32)
    edge_lane = lax.broadcasted_iota(I32, (8, DEV), 1)
    edge = jnp.where(edge_lane == 0, edges[0], jnp.where(edge_lane == 1, edges[1], edges[2]))
    edge_ref[...] = edge.astype(I32)


class Exchange:
    def __init__(self, axis, size, source, target, send, recv, peers=None, keep=True):
        self.axis, self.size, self.source, self.target = axis, size, source, target
        self.send, self.recv, self.keep = send, recv, keep
        self.me = lax.axis_index(axis)
        self.peers = peers if peers is not None else lambda k: lax.rem(self.me + k, size)

    def copy(self, k):
        peer = self.peers(k)
        return pltpu.make_async_remote_copy(
            src_ref=self.source(peer),
            dst_ref=self.target(self.me),
            send_sem=self.send.at[k],
            recv_sem=self.recv.at[k],
            device_id={self.axis: peer},
            device_id_type=pl.DeviceIdType.MESH,
        )

    def own(self):
        return pltpu.make_async_copy(self.source(self.me), self.target(self.me), self.recv.at[0])

    def start(self):
        def step(k, _):
            self.copy(k).start()
            return 0

        lax.fori_loop(1, self.size, step, 0)
        if self.keep:
            self.own().start()

    def wait_recv(self):
        def step(k, _):
            self.copy(k).wait_recv()
            return 0

        lax.fori_loop(1, self.size, step, 0)
        if self.keep:
            self.own().wait()

    def wait_send(self):
        def step(k, _):
            self.copy(k).wait_send()
            return 0

        lax.fori_loop(1, self.size, step, 0)


def greet(axes):
    barrier = pltpu.get_barrier_semaphore()
    for axis, size in axes:
        me = lax.axis_index(axis)

        def step(k, _, axis=axis, size=size, me=me):
            pl.semaphore_signal(
                barrier, inc=1, device_id={axis: lax.rem(me + k, size)}, device_id_type=pl.DeviceIdType.MESH
            )
            return 0

        lax.fori_loop(1, size, step, 0)


def spectrum_kernel(
    rcv_ref,
    src_ref,
    traces_ref,
    first_ref,
    second_ref,
    data_first_ref,
    data_second_ref,
    cell_rows_ref,
    count_ref,
    start_ref,
    list_ref,
    edge_ref,
    x_ref,
    table_ref,
    pick_ref,
    spec_ref,
    spread_ref,
    cell_send,
    cell_mid,
    cell_pack,
    cell_all,
    code_wide,
    first_send,
    first_mid,
    second_send,
    second_mid,
    load_sem,
    bin_send,
    bin_recv,
    freq_send,
    freq_recv,
    core_send,
    core_recv,
):
    def over_bin(slot, source, target):
        return Exchange("bin", 8, source, target, bin_send.at[slot], bin_recv.at[slot])

    def over_freq(slot, source, target):
        return Exchange("freq", 16, source, target, freq_send.at[slot], freq_recv.at[slot])

    bin_me = lax.axis_index("bin")
    core, x_me = lax.rem(bin_me, 2), bin_me // 2
    cell_freq = over_freq(0, lambda f: cell_send, lambda me: cell_mid.at[me])
    cell_x = Exchange(
        "bin",
        4,
        lambda b: cell_pack,
        lambda me: cell_all.at[core, x_me],
        bin_send.at[0],
        bin_recv.at[0],
        peers=lambda k: lax.rem(bin_me + 2 * k, 8),
    )
    cell_core = Exchange(
        "bin",
        2,
        lambda b: cell_all.at[core],
        lambda me: cell_all.at[core],
        core_send,
        core_recv,
        peers=lambda k: bin_me + 1 - 2 * core,
        keep=False,
    )
    first_bin = over_bin(1, lambda b: first_send.at[b], lambda me: first_mid.at[me])
    first_freq = over_freq(1, lambda f: first_mid.at[:, f], lambda me: data_first_ref.at[me])
    second_freq = over_freq(2, lambda f: second_send.at[f], lambda me: second_mid.at[me])
    second_bin = over_bin(2, lambda b: second_mid.at[:, b], lambda me: data_second_ref.at[me])

    def load_traces(m):
        at = pl.ds(m * 256, 256)
        return pltpu.make_async_copy(traces_ref.at[at], x_ref.at[at], load_sem.at[m])

    def load_table(h):
        return pltpu.make_async_copy((first_ref, second_ref)[h], table_ref.at[h], load_sem.at[4 + h])

    greet((("bin", 8), ("freq", 16)))
    load_table(0).start()
    for m in range(4):
        load_traces(m).start()
    load_table(1).start()
    carry, upper, row_i = index_work(rcv_ref, src_ref, pick_ref, cell_send, count_ref, start_ref)
    pl.semaphore_wait(pltpu.get_barrier_semaphore(), 22)
    cell_freq.start()

    def transform(h):
        load_table(h).wait()

        def rows(m, _):
            if h == 0:
                load_traces(m).wait()
            at = pl.ds(pl.multiple_of(m * 256, 256), 256)
            both = jnp.dot(x_ref[at, :], table_ref[h], preferred_element_type=F32)
            spec_ref[at, :] = (both[:, :256] + both[:, 256:]).astype(BF16)
            return 0

        lax.fori_loop(0, 4, rows, 0)

    def sort_rows():
        for half in range(2):
            q = half * 512
            rows = lax.dot_general(
                spec_ref[...], pick_ref[:, q : q + 512], (((0,), (0,)), ((), ())), preferred_element_type=F32
            )
            for blk in range(4):
                spread_ref[pl.ds(half * 4 + blk, 256, stride=8), :] = rows[:, blk * DEV : (blk + 1) * DEV]

    transform(0)
    sort_rows()
    for b in range(8):
        first_send[b] = spread_ref[b * 256 : (b + 1) * 256, :].reshape(16, 16, DEV).astype(BF16)
    cell_freq.wait_recv()
    cell_pack[...] = cell_mid[...].reshape(DEV, DEV).astype(jnp.int16)
    cell_x.start()
    first_bin.start()
    transform(1)
    sort_rows()
    for f in range(16):
        second_send[f] = spread_ref[f * 128 : (f + 1) * 128, :].reshape(8, 16, DEV).astype(BF16)
    second_freq.start()
    list_runs(carry, upper, row_i, list_ref, edge_ref)
    first_bin.wait_recv()
    first_freq.start()
    cell_x.wait_recv()
    cell_core.start()
    cell_core.wait_recv()
    for c in range(2):
        for x in range(4):
            at = (x * 2 + c) * DEV
            code_wide[at : at + DEV, :] = cell_all[c, x].astype(F32)
    stride = TR + 16
    for blk in range(8):
        code = code_wide[pl.ds(blk, DEV, stride=8), :].T.astype(I32)
        cell_rows_ref[blk * DEV : (blk + 1) * DEV, :] = (code >> 6).astype(F32)
        cell_rows_ref[stride + blk * DEV : stride + (blk + 1) * DEV, :] = (code & 63).astype(F32)
    for digit in range(2):
        cell_rows_ref[digit * stride + TR : (digit + 1) * stride, :] = jnp.zeros((16, DEV), F32)
    second_freq.wait_recv()
    second_bin.start()
    first_freq.wait_recv()
    second_bin.wait_recv()
    for part in (cell_freq, cell_x, cell_core, first_bin, first_freq, second_freq, second_bin):
        part.wait_send()


def layout_kernel(
    count_ref,
    start_ref,
    list_ref,
    edge_ref,
    first_ref,
    second_ref,
    cell_ref,
    dense_ref,
    first_wide,
    second_wide,
    rows_ref,
    raw_ref,
):
    stride = TR + 16
    for b in range(8):
        second_wide[b * 256 : (b + 1) * 256, :] = second_ref[b].reshape(256, DEV).astype(F32)
        for f in range(16):
            at = (b * 16 + f) * 16
            first_wide[at : at + 16, :] = first_ref[f, b].astype(F32)
    for blk in range(8):
        for part in range(2):
            pick = pl.ds(part * 8 + blk, DEV, stride=16)
            rows_ref[pl.ds(part * stride + blk * DEV, DEV), :] = first_wide[pick, :].T
            rows_ref[pl.ds((2 + part) * stride + blk * DEV, DEV), :] = second_wide[pick, :].T
    pad = jnp.zeros((16, DEV), F32)
    for comp in range(4):
        rows_ref[pl.ds(comp * stride + TR, 16), :] = pad

    sub32 = lax.broadcasted_iota(I32, (32, DEV), 0).astype(F32).astype(BF16)
    sub64 = lax.broadcasted_iota(I32, (64, DEV), 0).astype(F32).astype(BF16)
    one, zero = jnp.ones((), BF16), jnp.zeros((), BF16)

    def lay_out(run, size):
        count = count_ref[0, run]
        start = start_ref[0, run]
        left, right = [], []
        for j in range(size):
            at = start + j
            high = jnp.broadcast_to(cell_ref[pl.ds(at, 1), :], (16, DEV))
            high = jnp.where(j < count, high, -1.0).astype(BF16)
            hit = jnp.concatenate([high] * 2, axis=0) == sub32
            parts = []
            for comp in range(4):
                row = jnp.broadcast_to(rows_ref[pl.ds(comp * stride + at, 1), :], (16, DEV)).astype(BF16)
                parts.append(jnp.where(hit, jnp.concatenate([row] * 2, axis=0), zero))
            left.append(jnp.concatenate(parts, axis=0))
            low = jnp.broadcast_to(cell_ref[pl.ds(stride + at, 1), :], (16, DEV)).astype(BF16)
            right.append(jnp.where(jnp.concatenate([low] * 4, axis=0) == sub64, one, zero))
        raw_ref[run, :, 0:64] = lax.dot_general(
            jnp.concatenate(left, axis=1),
            jnp.concatenate(right, axis=1),
            (((1,), (1,)), ((), ())),
            preferred_element_type=F32,
        )

    begin = 0
    for kind, (size, together) in enumerate(((4, 32), (8, 32), (16, 16))):
        end = edge_ref[0, kind]

        def some_runs(step, _, begin=begin, end=end, size=size, together=together):
            for u in range(together):
                lay_out(list_ref[0, jnp.minimum(begin + step * together + u, end - 1)], size)
            return 0

        lax.fori_loop(0, (end - begin + together - 1) // together, some_runs, 0)
        begin = end

    top = lax.broadcasted_iota(I32, (8, DEV), 0) < 4
    left_half = lax.broadcasted_iota(I32, (8, DEV), 1) < 64

    def four_runs(group, _):
        for comp in range(4):
            at = pl.ds(pl.multiple_of(comp * ORDER + group * 16, 16), 16)
            for tile in range(4):
                sl = pl.ds(comp * 32 + 8 * tile, 8)
                merged = []
                for pair in range(2):
                    even = raw_ref[4 * group + 2 * pair, sl, :]
                    odd = raw_ref[4 * group + 2 * pair + 1, sl, :]
                    right = pltpu.roll(pltpu.roll(jnp.where(top, odd, even), 4, 0), 64, 1)
                    merged.append(jnp.where(left_half, jnp.where(top, even, odd), right))
                dense_ref[at, pl.ds(tile * DEV, DEV)] = jnp.concatenate(merged, axis=0).astype(BF16)
        return 0

    lax.fori_loop(0, DEV // 4, four_runs, 0, unroll=2)


def product_kernel(filt_ref, dense_ref, out_ref, hold_ref, block_ref, load_sem, send, recv):
    loads = []
    for i in range(2):
        part = pl.ds(2 * i * ORDER, 2 * ORDER)
        loads.append(pltpu.make_async_copy(dense_ref.at[part], hold_ref.at[part], load_sem.at[i]))
        loads[-1].start()
    mine = lax.axis_index("bin") * 2
    amplitude = 1.0 / math.sqrt(ORDER)
    greet((("bin", 8),))
    moves = [
        Exchange(
            "bin",
            8,
            lambda b, i=i: block_ref.at[b, i],
            lambda me, i=i: out_ref.at[:, me * 2 + i],
            send.at[i],
            recv.at[i],
        )
        for i in range(2)
    ]
    for i in range(2):
        loads[i].wait()
        real = hold_ref[pl.ds(2 * i * ORDER, ORDER), :]
        imag = hold_ref[pl.ds((2 * i + 1) * ORDER, ORDER), :]
        fr = filt_ref[0, mine + i]
        fi = filt_ref[1, mine + i]
        for t in range(2):
            cols = slice(t * 256, (t + 1) * 256)
            rc, ic = real[:, cols], imag[:, cols]
            dot = functools.partial(jnp.dot, preferred_element_type=F32)
            sr = dot(real, rc) - dot(imag, ic)
            si = dot(real, ic) + dot(imag, rc)
            outr = ((fr * sr - fi * si) * amplitude).astype(BF16)
            outi = ((fr * si + fi * sr) * amplitude).astype(BF16)
            for b in range(8):
                block_ref[b, i, 0, :, cols] = outr[b * 64 : (b + 1) * 64]
                block_ref[b, i, 1, :, cols] = outi[b * 64 : (b + 1) * 64]
        if i == 0:
            pl.semaphore_wait(pltpu.get_barrier_semaphore(), 7)
        moves[i].start()
    for move in moves:
        move.wait_recv()
        move.wait_send()


def hand_over(rows_ref, out_ref, hold_ref, sem):
    loads = [pltpu.make_async_copy(rows_ref.at[:, i], hold_ref.at[:, i], sem.at[0, i]) for i in range(16)]
    stores = [pltpu.make_async_copy(hold_ref.at[:, i], out_ref.at[:, i], sem.at[1, i]) for i in range(16)]
    for load in loads:
        load.start()
    for load, store in zip(loads, stores):
        load.wait()
        store.start()
    for store in stores:
        store.wait()


def local(traces, rcv_index, src_index, wave_filter):
    tables = dft_tables()
    params = pltpu.CompilerParams(vmem_limit_bytes=LIMIT)
    vmem = pl.BlockSpec(memory_space=pltpu.VMEM)
    smem = pl.BlockSpec(memory_space=pltpu.SMEM)
    anywhere = pl.BlockSpec(memory_space=pl.ANY)
    shape = jax.ShapeDtypeStruct
    small = shape((8, DEV), I32)
    dma = pltpu.SemaphoreType.DMA
    outgoing, middle = pltpu.VMEM((8, 16, 16, DEV), BF16), pltpu.VMEM((16, 8, 16, DEV), BF16)
    first, second, cells, count, start, listed, edge = pl.pallas_call(
        spectrum_kernel,
        in_specs=[vmem, vmem, anywhere, anywhere, anywhere],
        out_specs=(anywhere, anywhere, vmem, vmem, vmem, vmem, vmem),
        out_shape=(
            shape((16, 8, 16, DEV), BF16),
            shape((8, 16, 16, DEV), BF16),
            shape((2 * (TR + 16), DEV), F32),
            small,
            small,
            small,
            small,
        ),
        scratch_shapes=[
            pltpu.VMEM((TR, NT), BF16),
            pltpu.VMEM((2, NT, 4 * DEV), BF16),
            pltpu.VMEM((TR, TR), BF16),
            pltpu.VMEM((TR, 256), BF16),
            pltpu.VMEM((2048, DEV), F32),
            pltpu.VMEM((8, DEV), I32),
            pltpu.VMEM((16, 8, DEV), I32),
            pltpu.VMEM((DEV, DEV), jnp.int16),
            pltpu.VMEM((2, 4, DEV, DEV), jnp.int16),
            pltpu.VMEM((TR, DEV), F32),
            outgoing,
            outgoing,
            middle,
            middle,
            dma((6,)),
            dma((3, 8)),
            dma((3, 8)),
            dma((3, 16)),
            dma((3, 16)),
            dma((2,)),
            dma((2,)),
        ],
        compiler_params=pltpu.CompilerParams(vmem_limit_bytes=LIMIT, collective_id=1, has_side_effects=True),
        cost_estimate=pl.CostEstimate(flops=5 * 10**9, bytes_accessed=9 * 10**6, transcendentals=0),
        name="spectrum",
    )(rcv_index.reshape(8, DEV), src_index.reshape(8, DEV), traces, jnp.asarray(tables[0]), jnp.asarray(tables[1]))
    dense = pl.pallas_call(
        layout_kernel,
        in_specs=[smem, smem, smem, smem, vmem, vmem, vmem],
        out_specs=vmem,
        out_shape=shape((4 * ORDER, ORDER), BF16),
        scratch_shapes=[
            pltpu.VMEM((2048, DEV), F32),
            pltpu.VMEM((2048, DEV), F32),
            pltpu.VMEM((4 * (TR + 16), DEV), F32),
            pltpu.VMEM((DEV, DEV, DEV), F32),
        ],
        compiler_params=params,
        name="layout",
    )(count, start, listed, edge, first, second, cells)
    rows = pl.pallas_call(
        product_kernel,
        in_specs=[smem, anywhere],
        out_specs=anywhere,
        out_shape=shape((2, 16, 64, ORDER), BF16),
        scratch_shapes=[
            pltpu.VMEM((4 * ORDER, ORDER), BF16),
            pltpu.VMEM((8, 2, 2, 64, ORDER), BF16),
            dma((2,)),
            dma((2, 8)),
            dma((2, 8)),
        ],
        compiler_params=pltpu.CompilerParams(vmem_limit_bytes=LIMIT, collective_id=2, has_side_effects=True),
        name="product",
    )(wave_filter, dense)
    return pl.pallas_call(
        hand_over,
        in_specs=[anywhere],
        out_specs=anywhere,
        out_shape=shape((2, 16, 64, ORDER), BF16),
        scratch_shapes=[pltpu.VMEM((2, 16, 64, ORDER), BF16), dma((2, 16))],
        compiler_params=params,
        name="hand_over",
    )(rows)


def solution(mesh):
    placed = (P(("bin", "freq"), None), P(("bin", "freq")), P(("bin", "freq")), P(None, "freq"))
    return jax.shard_map(
        local, mesh=mesh, in_specs=placed, out_specs=P(None, "freq", "bin", None), check_vma=False
    )
```

```python
import functools
import math

import jax
import jax.numpy as jnp
import numpy as np
from jax import lax
from jax.experimental import pallas as pl
from jax.experimental.pallas import tpu as pltpu
from jax.sharding import PartitionSpec as P
import ml_dtypes

ORDER = 512
NT = 2048
NF = 256
DEV = 128
TR = 1024
F32 = jnp.float32
BF16 = jnp.bfloat16
I32 = jnp.int32
LIMIT = 56 * 1024 * 1024


def dft_tables():
    bins, freqs, part = np.meshgrid(np.arange(8), np.arange(16), np.arange(2), indexing="ij")
    first = freqs * 16 + bins * 2
    order = (1, 0, 2)
    freq = np.concatenate([first.reshape(-1), (first + 1).transpose(order).reshape(-1)])
    part = np.concatenate([part.reshape(-1), part.transpose(order).reshape(-1)])
    phase = (np.arange(NT)[:, None] * freq[None, :]) % NT
    angle = 2.0 * np.pi / NT * phase
    table = np.where(part[None, :] == 0, np.cos(angle), -np.sin(angle)) / math.sqrt(NT)
    high = table.astype(ml_dtypes.bfloat16)
    low = (table - high.astype(np.float64)).astype(ml_dtypes.bfloat16)
    return [np.concatenate([high[:, h : h + 256], low[:, h : h + 256]], axis=1) for h in (0, 256)]


def index_work(rcv_ref, src_ref, pick_ref, cell_ref, count_ref, start_ref):
    lane = lax.broadcasted_iota(I32, (TR, DEV), 1)
    row_i = lax.broadcasted_iota(I32, (DEV, DEV), 0)
    col_i = lax.broadcasted_iota(I32, (DEV, DEV), 1)
    lower = (col_i < row_i).astype(BF16)
    upper = (row_i < col_i).astype(BF16)
    same = row_i == col_i
    rcv = rcv_ref[...]
    src = src_ref[...]
    run = (rcv >> 2).astype(F32)
    columns = []
    for blk in range(TR // DEV):
        spread = jnp.where(same, jnp.broadcast_to(run[blk : blk + 1, :], (DEV, DEV)), 0.0)
        columns.append(jnp.sum(spread, axis=1, keepdims=True))
    member = (jnp.concatenate(columns, axis=0).astype(I32) == lane).astype(F32)
    carry = jnp.zeros((1, DEV), F32)
    ranks = []
    for blk in range(TR // DEV):
        m = member[blk * DEV : (blk + 1) * DEV]
        ranks.append(jnp.dot(lower, m.astype(BF16), preferred_element_type=F32) + carry)
        carry = carry + jnp.sum(m, axis=0, keepdims=True)
    rank_all = jnp.concatenate(ranks, axis=0)
    counts8 = jnp.broadcast_to(carry, (8, DEV))
    start = jnp.dot(counts8.astype(BF16), upper, preferred_element_type=F32)
    place = jnp.sum(member * (rank_all + start[0:1]), axis=1, keepdims=True).astype(I32)
    count_ref[...] = counts8.astype(I32)
    start_ref[...] = start.astype(I32)
    pick_ref[...] = (place == lax.broadcasted_iota(I32, (TR, TR), 1)).astype(F32).astype(BF16)
    half = ((src >> 6) + (rcv >> 2)) & 1
    high = ((src >> 7) * 8 + half * 4 + (rcv & 3)).astype(F32)
    low = (src & 63).astype(F32)
    flat = [jnp.concatenate([v[blk : blk + 1, :] for blk in range(TR // DEV)], axis=1) for v in (high, low)]
    digits = jnp.concatenate([jnp.broadcast_to(v, (8, TR)) for v in flat], axis=0).astype(BF16)
    both = jnp.dot(digits, pick_ref[...], preferred_element_type=F32)
    for blk in range(TR // DEV):
        cols = slice(blk * DEV, (blk + 1) * DEV)
        cell_ref[blk : blk + 1, :] = (both[0:1, cols] * 64.0 + both[8:9, cols]).astype(I32)
    return carry, upper, row_i


def list_runs(carry, upper, row_i, list_ref, edge_ref):
    cls = [carry <= 4.0, (carry > 4.0) & (carry <= 8.0), carry > 8.0]
    base = jnp.zeros((1, 1), F32)
    spot = jnp.zeros((1, DEV), F32)
    edges = []
    for kind in cls:
        ind = kind.astype(F32)
        before = jnp.dot(jnp.broadcast_to(ind, (8, DEV)).astype(BF16), upper, preferred_element_type=F32)[0:1]
        spot = spot + ind * (before + base)
        base = base + jnp.sum(ind, axis=1, keepdims=True)
        edges.append(base)
    here = (jnp.broadcast_to(spot, (DEV, DEV)) == row_i.astype(F32)).astype(BF16)
    names = lax.broadcasted_iota(I32, (8, DEV), 1).astype(F32).astype(BF16)
    list_ref[...] = lax.dot_general(
        names, here, (((1,), (1,)), ((), ())), preferred_element_type=F32
    ).astype(I32)
    edge_lane = lax.broadcasted_iota(I32, (8, DEV), 1)
    edge = jnp.where(edge_lane == 0, edges[0], jnp.where(edge_lane == 1, edges[1], edges[2]))
    edge_ref[...] = edge.astype(I32)


class Exchange:
    def __init__(self, axis, size, source, target, send, recv, peers=None, keep=True):
        self.axis, self.size, self.source, self.target = axis, size, source, target
        self.send, self.recv, self.keep = send, recv, keep
        self.me = lax.axis_index(axis)
        self.peers = peers if peers is not None else lambda k: lax.rem(self.me + k, size)

    def copy(self, k):
        peer = self.peers(k)
        return pltpu.make_async_remote_copy(
            src_ref=self.source(peer),
            dst_ref=self.target(self.me),
            send_sem=self.send.at[k],
            recv_sem=self.recv.at[k],
            device_id={self.axis: peer},
            device_id_type=pl.DeviceIdType.MESH,
        )

    def own(self):
        return pltpu.make_async_copy(self.source(self.me), self.target(self.me), self.recv.at[0])

    def start(self):
        def step(k, _):
            self.copy(k).start()
            return 0

        lax.fori_loop(1, self.size, step, 0)
        if self.keep:
            self.own().start()

    def wait_recv(self):
        def step(k, _):
            self.copy(k).wait_recv()
            return 0

        lax.fori_loop(1, self.size, step, 0)
        if self.keep:
            self.own().wait()

    def wait_send(self):
        def step(k, _):
            self.copy(k).wait_send()
            return 0

        lax.fori_loop(1, self.size, step, 0)


def far_first(k):
    me = lax.axis_index("bin")
    turn = (k - 1) // 2
    away = jnp.where(turn == 0, 2, jnp.where(turn == 1, 1, jnp.where(turn == 2, 3, 0)))
    return lax.rem(me // 2 + away, 4) * 2 + lax.rem(me + k, 2)


def greet(axes):
    barrier = pltpu.get_barrier_semaphore()
    for axis, size in axes:
        me = lax.axis_index(axis)

        def step(k, _, axis=axis, size=size, me=me):
            pl.semaphore_signal(
                barrier, inc=1, device_id={axis: lax.rem(me + k, size)}, device_id_type=pl.DeviceIdType.MESH
            )
            return 0

        lax.fori_loop(1, size, step, 0)


def spectrum_kernel(
    rcv_ref,
    src_ref,
    traces_ref,
    first_ref,
    second_ref,
    data_first_ref,
    data_second_ref,
    cell_rows_ref,
    count_ref,
    start_ref,
    list_ref,
    edge_ref,
    x_ref,
    table_ref,
    pick_ref,
    spec_ref,
    spread_ref,
    cell_send,
    cell_mid,
    cell_pack,
    cell_all,
    code_wide,
    first_send,
    first_mid,
    second_send,
    second_mid,
    load_sem,
    bin_send,
    bin_recv,
    freq_send,
    freq_recv,
    core_send,
    core_recv,
):
    def over_bin(slot, source, target):
        return Exchange("bin", 8, source, target, bin_send.at[slot], bin_recv.at[slot])

    def over_freq(slot, source, target):
        return Exchange("freq", 16, source, target, freq_send.at[slot], freq_recv.at[slot])

    bin_me = lax.axis_index("bin")
    core, x_me = lax.rem(bin_me, 2), bin_me // 2
    cell_freq = over_freq(0, lambda f: cell_send, lambda me: cell_mid.at[me])
    cell_x = Exchange(
        "bin",
        4,
        lambda b: cell_pack,
        lambda me: cell_all.at[core, x_me],
        bin_send.at[0],
        bin_recv.at[0],
        peers=lambda k: lax.rem(bin_me + 2 * k, 8),
    )
    cell_core = Exchange(
        "bin",
        2,
        lambda b: cell_all.at[core],
        lambda me: cell_all.at[core],
        core_send,
        core_recv,
        peers=lambda k: bin_me + 1 - 2 * core,
        keep=False,
    )
    first_bin = over_bin(1, lambda b: first_send.at[b], lambda me: first_mid.at[me])
    first_freq = over_freq(1, lambda f: first_mid.at[:, f], lambda me: data_first_ref.at[me])
    second_freq = over_freq(2, lambda f: second_send.at[f], lambda me: second_mid.at[me])
    second_bin = over_bin(2, lambda b: second_mid.at[:, b], lambda me: data_second_ref.at[me])

    def load_traces(m):
        at = pl.ds(m * 256, 256)
        return pltpu.make_async_copy(traces_ref.at[at], x_ref.at[at], load_sem.at[m])

    def load_table(h):
        return pltpu.make_async_copy((first_ref, second_ref)[h], table_ref.at[h], load_sem.at[4 + h])

    greet((("bin", 8), ("freq", 16)))
    load_table(0).start()
    for m in range(4):
        load_traces(m).start()
    load_table(1).start()
    carry, upper, row_i = index_work(rcv_ref, src_ref, pick_ref, cell_send, count_ref, start_ref)
    pl.semaphore_wait(pltpu.get_barrier_semaphore(), 22)
    cell_freq.start()

    def transform(h):
        load_table(h).wait()

        def rows(m, _):
            if h == 0:
                load_traces(m).wait()
            at = pl.ds(pl.multiple_of(m * 256, 256), 256)
            both = jnp.dot(x_ref[at, :], table_ref[h], preferred_element_type=F32)
            spec_ref[at, :] = (both[:, :256] + both[:, 256:]).astype(BF16)
            return 0

        lax.fori_loop(0, 4, rows, 0)

    def sort_rows():
        for half in range(2):
            q = half * 512
            rows = lax.dot_general(
                spec_ref[...], pick_ref[:, q : q + 512], (((0,), (0,)), ((), ())), preferred_element_type=F32
            )
            for blk in range(4):
                spread_ref[pl.ds(half * 4 + blk, 256, stride=8), :] = rows[:, blk * DEV : (blk + 1) * DEV]

    transform(0)
    sort_rows()
    for b in range(8):
        first_send[b] = spread_ref[b * 256 : (b + 1) * 256, :].reshape(16, 16, DEV).astype(BF16)
    cell_freq.wait_recv()
    cell_pack[...] = cell_mid[...].reshape(DEV, DEV).astype(jnp.int16)
    cell_x.start()
    first_bin.start()
    transform(1)
    sort_rows()
    for f in range(16):
        second_send[f] = spread_ref[f * 128 : (f + 1) * 128, :].reshape(8, 16, DEV).astype(BF16)
    second_freq.start()
    list_runs(carry, upper, row_i, list_ref, edge_ref)
    first_bin.wait_recv()
    first_freq.start()
    cell_x.wait_recv()
    cell_core.start()
    cell_core.wait_recv()
    for c in range(2):
        for x in range(4):
            at = (x * 2 + c) * DEV
            code_wide[at : at + DEV, :] = cell_all[c, x].astype(F32)
    stride = TR + 16
    for blk in range(8):
        code = code_wide[pl.ds(blk, DEV, stride=8), :].T.astype(I32)
        cell_rows_ref[blk * DEV : (blk + 1) * DEV, :] = (code >> 6).astype(F32)
        cell_rows_ref[stride + blk * DEV : stride + (blk + 1) * DEV, :] = (code & 63).astype(F32)
    for digit in range(2):
        cell_rows_ref[digit * stride + TR : (digit + 1) * stride, :] = jnp.zeros((16, DEV), F32)
    second_freq.wait_recv()
    second_bin.start()
    first_freq.wait_recv()
    second_bin.wait_recv()
    for part in (cell_freq, cell_x, cell_core, first_bin, first_freq, second_freq, second_bin):
        part.wait_send()


def layout_kernel(
    count_ref,
    start_ref,
    list_ref,
    edge_ref,
    first_ref,
    second_ref,
    cell_ref,
    dense_ref,
    first_wide,
    second_wide,
    rows_ref,
    raw_ref,
):
    stride = TR + 16
    for b in range(8):
        second_wide[b * 256 : (b + 1) * 256, :] = second_ref[b].reshape(256, DEV).astype(F32)
        for f in range(16):
            at = (b * 16 + f) * 16
            first_wide[at : at + 16, :] = first_ref[f, b].astype(F32)
    for blk in range(8):
        for part in range(2):
            pick = pl.ds(part * 8 + blk, DEV, stride=16)
            rows_ref[pl.ds(part * stride + blk * DEV, DEV), :] = first_wide[pick, :].T
            rows_ref[pl.ds((2 + part) * stride + blk * DEV, DEV), :] = second_wide[pick, :].T
    pad = jnp.zeros((16, DEV), F32)
    for comp in range(4):
        rows_ref[pl.ds(comp * stride + TR, 16), :] = pad

    sub32 = lax.broadcasted_iota(I32, (32, DEV), 0).astype(F32).astype(BF16)
    sub64 = lax.broadcasted_iota(I32, (64, DEV), 0).astype(F32).astype(BF16)
    one, zero = jnp.ones((), BF16), jnp.zeros((), BF16)

    def lay_out(run, size):
        count = count_ref[0, run]
        start = start_ref[0, run]
        left, right = [], []
        for j in range(size):
            at = start + j
            high = jnp.broadcast_to(cell_ref[pl.ds(at, 1), :], (16, DEV))
            high = jnp.where(j < count, high, -1.0).astype(BF16)
            hit = jnp.concatenate([high] * 2, axis=0) == sub32
            parts = []
            for comp in range(4):
                row = jnp.broadcast_to(rows_ref[pl.ds(comp * stride + at, 1), :], (16, DEV)).astype(BF16)
                parts.append(jnp.where(hit, jnp.concatenate([row] * 2, axis=0), zero))
            left.append(jnp.concatenate(parts, axis=0))
            low = jnp.broadcast_to(cell_ref[pl.ds(stride + at, 1), :], (16, DEV)).astype(BF16)
            right.append(jnp.where(jnp.concatenate([low] * 4, axis=0) == sub64, one, zero))
        raw_ref[run, :, 0:64] = lax.dot_general(
            jnp.concatenate(left, axis=1),
            jnp.concatenate(right, axis=1),
            (((1,), (1,)), ((), ())),
            preferred_element_type=F32,
        )

    begin = 0
    for kind, (size, together) in enumerate(((4, 32), (8, 32), (16, 16))):
        end = edge_ref[0, kind]

        def some_runs(step, _, begin=begin, end=end, size=size, together=together):
            for u in range(together):
                lay_out(list_ref[0, jnp.minimum(begin + step * together + u, end - 1)], size)
            return 0

        lax.fori_loop(0, (end - begin + together - 1) // together, some_runs, 0)
        begin = end

    top = lax.broadcasted_iota(I32, (8, DEV), 0) < 4
    left_half = lax.broadcasted_iota(I32, (8, DEV), 1) < 64

    def four_runs(group, _):
        for comp in range(4):
            at = pl.ds(pl.multiple_of(comp * ORDER + group * 16, 16), 16)
            for tile in range(4):
                sl = pl.ds(comp * 32 + 8 * tile, 8)
                merged = []
                for pair in range(2):
                    even = raw_ref[4 * group + 2 * pair, sl, :]
                    odd = raw_ref[4 * group + 2 * pair + 1, sl, :]
                    right = pltpu.roll(pltpu.roll(jnp.where(top, odd, even), 4, 0), 64, 1)
                    merged.append(jnp.where(left_half, jnp.where(top, even, odd), right))
                dense_ref[at, pl.ds(tile * DEV, DEV)] = jnp.concatenate(merged, axis=0).astype(BF16)
        return 0

    lax.fori_loop(0, DEV // 4, four_runs, 0, unroll=2)


def product_kernel(filt_ref, dense_ref, out_ref, hold_ref, block_ref, load_sem, send, recv):
    loads = []
    for i in range(2):
        part = pl.ds(2 * i * ORDER, 2 * ORDER)
        loads.append(pltpu.make_async_copy(dense_ref.at[part], hold_ref.at[part], load_sem.at[i]))
        loads[-1].start()
    mine = lax.axis_index("bin") * 2
    amplitude = 1.0 / math.sqrt(ORDER)
    greet((("bin", 8),))
    moves = [
        Exchange(
            "bin",
            8,
            lambda b, i=i: block_ref.at[b, i],
            lambda me, i=i: out_ref.at[:, me * 2 + i],
            send.at[i],
            recv.at[i],
            peers=far_first,
        )
        for i in range(2)
    ]
    for i in range(2):
        loads[i].wait()
        real = hold_ref[pl.ds(2 * i * ORDER, ORDER), :]
        imag = hold_ref[pl.ds((2 * i + 1) * ORDER, ORDER), :]
        fr = filt_ref[0, mine + i]
        fi = filt_ref[1, mine + i]
        for t in range(2):
            cols = slice(t * 256, (t + 1) * 256)
            rc, ic = real[:, cols], imag[:, cols]
            dot = functools.partial(jnp.dot, preferred_element_type=F32)
            sr = dot(real, rc) - dot(imag, ic)
            si = dot(real, ic) + dot(imag, rc)
            outr = ((fr * sr - fi * si) * amplitude).astype(BF16)
            outi = ((fr * si + fi * sr) * amplitude).astype(BF16)
            for b in range(8):
                block_ref[b, i, 0, :, cols] = outr[b * 64 : (b + 1) * 64]
                block_ref[b, i, 1, :, cols] = outi[b * 64 : (b + 1) * 64]
        if i == 0:
            pl.semaphore_wait(pltpu.get_barrier_semaphore(), 7)
        moves[i].start()
    for move in moves:
        move.wait_recv()
        move.wait_send()


def hand_over(rows_ref, out_ref, hold_ref, sem):
    loads = [pltpu.make_async_copy(rows_ref.at[:, i], hold_ref.at[:, i], sem.at[0, i]) for i in range(16)]
    stores = [pltpu.make_async_copy(hold_ref.at[:, i], out_ref.at[:, i], sem.at[1, i]) for i in range(16)]
    for load in loads:
        load.start()
    for load, store in zip(loads, stores):
        load.wait()
        store.start()
    for store in stores:
        store.wait()


def local(traces, rcv_index, src_index, wave_filter):
    tables = dft_tables()
    params = pltpu.CompilerParams(vmem_limit_bytes=LIMIT)
    vmem = pl.BlockSpec(memory_space=pltpu.VMEM)
    smem = pl.BlockSpec(memory_space=pltpu.SMEM)
    anywhere = pl.BlockSpec(memory_space=pl.ANY)
    shape = jax.ShapeDtypeStruct
    small = shape((8, DEV), I32)
    dma = pltpu.SemaphoreType.DMA
    outgoing, middle = pltpu.VMEM((8, 16, 16, DEV), BF16), pltpu.VMEM((16, 8, 16, DEV), BF16)
    first, second, cells, count, start, listed, edge = pl.pallas_call(
        spectrum_kernel,
        in_specs=[vmem, vmem, anywhere, anywhere, anywhere],
        out_specs=(anywhere, anywhere, vmem, vmem, vmem, vmem, vmem),
        out_shape=(
            shape((16, 8, 16, DEV), BF16),
            shape((8, 16, 16, DEV), BF16),
            shape((2 * (TR + 16), DEV), F32),
            small,
            small,
            small,
            small,
        ),
        scratch_shapes=[
            pltpu.VMEM((TR, NT), BF16),
            pltpu.VMEM((2, NT, 4 * DEV), BF16),
            pltpu.VMEM((TR, TR), BF16),
            pltpu.VMEM((TR, 256), BF16),
            pltpu.VMEM((2048, DEV), F32),
            pltpu.VMEM((8, DEV), I32),
            pltpu.VMEM((16, 8, DEV), I32),
            pltpu.VMEM((DEV, DEV), jnp.int16),
            pltpu.VMEM((2, 4, DEV, DEV), jnp.int16),
            pltpu.VMEM((TR, DEV), F32),
            outgoing,
            outgoing,
            middle,
            middle,
            dma((6,)),
            dma((3, 8)),
            dma((3, 8)),
            dma((3, 16)),
            dma((3, 16)),
            dma((2,)),
            dma((2,)),
        ],
        compiler_params=pltpu.CompilerParams(vmem_limit_bytes=LIMIT, collective_id=1, has_side_effects=True),
        cost_estimate=pl.CostEstimate(flops=5 * 10**9, bytes_accessed=9 * 10**6, transcendentals=0),
        name="spectrum",
    )(rcv_index.reshape(8, DEV), src_index.reshape(8, DEV), traces, jnp.asarray(tables[0]), jnp.asarray(tables[1]))
    dense = pl.pallas_call(
        layout_kernel,
        in_specs=[smem, smem, smem, smem, vmem, vmem, vmem],
        out_specs=vmem,
        out_shape=shape((4 * ORDER, ORDER), BF16),
        scratch_shapes=[
            pltpu.VMEM((2048, DEV), F32),
            pltpu.VMEM((2048, DEV), F32),
            pltpu.VMEM((4 * (TR + 16), DEV), F32),
            pltpu.VMEM((DEV, DEV, DEV), F32),
        ],
        compiler_params=params,
        name="layout",
    )(count, start, listed, edge, first, second, cells)
    rows = pl.pallas_call(
        product_kernel,
        in_specs=[smem, anywhere],
        out_specs=anywhere,
        out_shape=shape((2, 16, 64, ORDER), BF16),
        scratch_shapes=[
            pltpu.VMEM((4 * ORDER, ORDER), BF16),
            pltpu.VMEM((8, 2, 2, 64, ORDER), BF16),
            dma((2,)),
            dma((2, 8)),
            dma((2, 8)),
        ],
        compiler_params=pltpu.CompilerParams(vmem_limit_bytes=LIMIT, collective_id=2, has_side_effects=True),
        name="product",
    )(wave_filter, dense)
    return pl.pallas_call(
        hand_over,
        in_specs=[anywhere],
        out_specs=anywhere,
        out_shape=shape((2, 16, 64, ORDER), BF16),
        scratch_shapes=[pltpu.VMEM((2, 16, 64, ORDER), BF16), dma((2, 16))],
        compiler_params=params,
        name="hand_over",
    )(rows)


def solution(mesh):
    placed = (P(("bin", "freq"), None), P(("bin", "freq")), P(("bin", "freq")), P(None, "freq"))
    return jax.shard_map(
        local, mesh=mesh, in_specs=placed, out_specs=P(None, "freq", "bin", None), check_vma=False
    )
```

```python
import functools
import math

import jax
import jax.numpy as jnp
import numpy as np
from jax import lax
from jax.experimental import pallas as pl
from jax.experimental.pallas import tpu as pltpu
from jax.sharding import PartitionSpec as P
import ml_dtypes

ORDER = 512
NT = 2048
NF = 256
DEV = 128
TR = 1024
F32 = jnp.float32
BF16 = jnp.bfloat16
I32 = jnp.int32
LIMIT = 56 * 1024 * 1024


def dft_tables():
    bins, freqs, part = np.meshgrid(np.arange(8), np.arange(16), np.arange(2), indexing="ij")
    first = freqs * 16 + bins * 2
    order = (1, 0, 2)
    freq = np.concatenate([first.reshape(-1), (first + 1).transpose(order).reshape(-1)])
    part = np.concatenate([part.reshape(-1), part.transpose(order).reshape(-1)])
    phase = (np.arange(NT)[:, None] * freq[None, :]) % NT
    angle = 2.0 * np.pi / NT * phase
    table = np.where(part[None, :] == 0, np.cos(angle), -np.sin(angle)) / math.sqrt(NT)
    high = table.astype(ml_dtypes.bfloat16)
    low = (table - high.astype(np.float64)).astype(ml_dtypes.bfloat16)
    return [np.concatenate([high[:, h : h + 256], low[:, h : h + 256]], axis=1) for h in (0, 256)]


def index_work(rcv_ref, src_ref, pick_ref, cell_ref, count_ref, start_ref):
    lane = lax.broadcasted_iota(I32, (TR, DEV), 1)
    row_i = lax.broadcasted_iota(I32, (DEV, DEV), 0)
    col_i = lax.broadcasted_iota(I32, (DEV, DEV), 1)
    lower = (col_i < row_i).astype(BF16)
    upper = (row_i < col_i).astype(BF16)
    same = row_i == col_i
    rcv = rcv_ref[...]
    src = src_ref[...]
    run = (rcv >> 2).astype(F32)
    columns = []
    for blk in range(TR // DEV):
        spread = jnp.where(same, jnp.broadcast_to(run[blk : blk + 1, :], (DEV, DEV)), 0.0)
        columns.append(jnp.sum(spread, axis=1, keepdims=True))
    member = (jnp.concatenate(columns, axis=0).astype(I32) == lane).astype(F32)
    carry = jnp.zeros((1, DEV), F32)
    ranks = []
    for blk in range(TR // DEV):
        m = member[blk * DEV : (blk + 1) * DEV]
        ranks.append(jnp.dot(lower, m.astype(BF16), preferred_element_type=F32) + carry)
        carry = carry + jnp.sum(m, axis=0, keepdims=True)
    rank_all = jnp.concatenate(ranks, axis=0)
    counts8 = jnp.broadcast_to(carry, (8, DEV))
    start = jnp.dot(counts8.astype(BF16), upper, preferred_element_type=F32)
    place = jnp.sum(member * (rank_all + start[0:1]), axis=1, keepdims=True).astype(I32)
    count_ref[...] = counts8.astype(I32)
    start_ref[...] = start.astype(I32)
    pick_ref[...] = (place == lax.broadcasted_iota(I32, (TR, TR), 1)).astype(F32).astype(BF16)
    half = ((src >> 6) + (rcv >> 2)) & 1
    high = ((src >> 7) * 8 + half * 4 + (rcv & 3)).astype(F32)
    low = (src & 63).astype(F32)
    flat = [jnp.concatenate([v[blk : blk + 1, :] for blk in range(TR // DEV)], axis=1) for v in (high, low)]
    digits = jnp.concatenate([jnp.broadcast_to(v, (8, TR)) for v in flat], axis=0).astype(BF16)
    both = jnp.dot(digits, pick_ref[...], preferred_element_type=F32)
    for blk in range(TR // DEV):
        cols = slice(blk * DEV, (blk + 1) * DEV)
        cell_ref[blk : blk + 1, :] = (both[0:1, cols] * 64.0 + both[8:9, cols]).astype(I32)
    return carry, upper, row_i


def list_runs(carry, upper, row_i, list_ref, edge_ref):
    cls = [carry <= 4.0, (carry > 4.0) & (carry <= 8.0), carry > 8.0]
    base = jnp.zeros((1, 1), F32)
    spot = jnp.zeros((1, DEV), F32)
    edges = []
    for kind in cls:
        ind = kind.astype(F32)
        before = jnp.dot(jnp.broadcast_to(ind, (8, DEV)).astype(BF16), upper, preferred_element_type=F32)[0:1]
        spot = spot + ind * (before + base)
        base = base + jnp.sum(ind, axis=1, keepdims=True)
        edges.append(base)
    here = (jnp.broadcast_to(spot, (DEV, DEV)) == row_i.astype(F32)).astype(BF16)
    names = lax.broadcasted_iota(I32, (8, DEV), 1).astype(F32).astype(BF16)
    list_ref[...] = lax.dot_general(
        names, here, (((1,), (1,)), ((), ())), preferred_element_type=F32
    ).astype(I32)
    edge_lane = lax.broadcasted_iota(I32, (8, DEV), 1)
    edge = jnp.where(edge_lane == 0, edges[0], jnp.where(edge_lane == 1, edges[1], edges[2]))
    edge_ref[...] = edge.astype(I32)


class Exchange:
    def __init__(self, axis, size, source, target, send, recv, peers=None, keep=True):
        self.axis, self.size, self.source, self.target = axis, size, source, target
        self.send, self.recv, self.keep = send, recv, keep
        self.me = lax.axis_index(axis)
        self.peers = peers if peers is not None else lambda k: lax.rem(self.me + k, size)

    def copy(self, k):
        peer = self.peers(k)
        return pltpu.make_async_remote_copy(
            src_ref=self.source(peer),
            dst_ref=self.target(self.me),
            send_sem=self.send.at[k],
            recv_sem=self.recv.at[k],
            device_id={self.axis: peer},
            device_id_type=pl.DeviceIdType.MESH,
        )

    def own(self):
        return pltpu.make_async_copy(self.source(self.me), self.target(self.me), self.recv.at[0])

    def start(self):
        def step(k, _):
            self.copy(k).start()
            return 0

        if self.axis == "freq":
            for k in FAR_FIRST:
                step(k, 0)
        else:
            lax.fori_loop(1, self.size, step, 0)
        if self.keep:
            self.own().start()

    def wait_recv(self):
        def step(k, _):
            self.copy(k).wait_recv()
            return 0

        lax.fori_loop(1, self.size, step, 0)
        if self.keep:
            self.own().wait()

    def wait_send(self):
        def step(k, _):
            self.copy(k).wait_send()
            return 0

        lax.fori_loop(1, self.size, step, 0)


def far_first(k):
    me = lax.axis_index("bin")
    turn = (k - 1) // 2
    away = jnp.where(turn == 0, 2, jnp.where(turn == 1, 1, jnp.where(turn == 2, 3, 0)))
    return lax.rem(me // 2 + away, 4) * 2 + lax.rem(me + k, 2)


def turned(k):
    me = lax.axis_index("freq")
    return lax.rem(me // 4 + k // 4, 4) * 4 + lax.rem(me + lax.rem(k, 4), 4)


FAR_FIRST = (10, 9, 11, 6, 14, 8, 2, 5, 7, 13, 15, 1, 3, 4, 12)


def greet(axes):
    barrier = pltpu.get_barrier_semaphore()
    for axis, size in axes:
        me = lax.axis_index(axis)

        def step(k, _, axis=axis, size=size, me=me):
            pl.semaphore_signal(
                barrier, inc=1, device_id={axis: lax.rem(me + k, size)}, device_id_type=pl.DeviceIdType.MESH
            )
            return 0

        lax.fori_loop(1, size, step, 0)


def spectrum_kernel(
    rcv_ref,
    src_ref,
    traces_ref,
    first_ref,
    second_ref,
    data_first_ref,
    data_second_ref,
    cell_rows_ref,
    count_ref,
    start_ref,
    list_ref,
    edge_ref,
    x_ref,
    table_ref,
    pick_ref,
    spec_ref,
    spread_ref,
    cell_send,
    cell_mid,
    cell_pack,
    cell_all,
    code_wide,
    first_send,
    first_mid,
    second_send,
    second_mid,
    load_sem,
    bin_send,
    bin_recv,
    freq_send,
    freq_recv,
    core_send,
    core_recv,
):
    def over_bin(slot, source, target):
        return Exchange("bin", 8, source, target, bin_send.at[slot], bin_recv.at[slot])

    def over_freq(slot, source, target):
        return Exchange("freq", 16, source, target, freq_send.at[slot], freq_recv.at[slot], peers=turned)

    bin_me = lax.axis_index("bin")
    core, x_me = lax.rem(bin_me, 2), bin_me // 2
    cell_freq = over_freq(0, lambda f: cell_send, lambda me: cell_mid.at[me])
    cell_x = Exchange(
        "bin",
        4,
        lambda b: cell_pack,
        lambda me: cell_all.at[core, x_me],
        bin_send.at[0],
        bin_recv.at[0],
        peers=lambda k: lax.rem(bin_me + 2 * k, 8),
    )
    cell_core = Exchange(
        "bin",
        2,
        lambda b: cell_all.at[core],
        lambda me: cell_all.at[core],
        core_send,
        core_recv,
        peers=lambda k: bin_me + 1 - 2 * core,
        keep=False,
    )
    first_bin = over_bin(1, lambda b: first_send.at[b], lambda me: first_mid.at[me])
    first_freq = over_freq(1, lambda f: first_mid.at[:, f], lambda me: data_first_ref.at[me])
    second_freq = over_freq(2, lambda f: second_send.at[f], lambda me: second_mid.at[me])
    second_bin = over_bin(2, lambda b: second_mid.at[:, b], lambda me: data_second_ref.at[me])

    def load_traces(m):
        at = pl.ds(m * 256, 256)
        return pltpu.make_async_copy(traces_ref.at[at], x_ref.at[at], load_sem.at[m])

    def load_table(h):
        return pltpu.make_async_copy((first_ref, second_ref)[h], table_ref.at[h], load_sem.at[4 + h])

    greet((("bin", 8), ("freq", 16)))
    load_table(0).start()
    for m in range(4):
        load_traces(m).start()
    load_table(1).start()
    carry, upper, row_i = index_work(rcv_ref, src_ref, pick_ref, cell_send, count_ref, start_ref)
    pl.semaphore_wait(pltpu.get_barrier_semaphore(), 22)
    cell_freq.start()

    def transform(h):
        load_table(h).wait()

        def rows(m, _):
            if h == 0:
                load_traces(m).wait()
            at = pl.ds(pl.multiple_of(m * 256, 256), 256)
            both = jnp.dot(x_ref[at, :], table_ref[h], preferred_element_type=F32)
            spec_ref[at, :] = (both[:, :256] + both[:, 256:]).astype(BF16)
            return 0

        lax.fori_loop(0, 4, rows, 0)

    def sort_rows():
        for half in range(2):
            q = half * 512
            rows = lax.dot_general(
                spec_ref[...], pick_ref[:, q : q + 512], (((0,), (0,)), ((), ())), preferred_element_type=F32
            )
            for blk in range(4):
                spread_ref[pl.ds(half * 4 + blk, 256, stride=8), :] = rows[:, blk * DEV : (blk + 1) * DEV]

    transform(0)
    sort_rows()
    for b in range(8):
        first_send[b] = spread_ref[b * 256 : (b + 1) * 256, :].reshape(16, 16, DEV).astype(BF16)
    cell_freq.wait_recv()
    cell_pack[...] = cell_mid[...].reshape(DEV, DEV).astype(jnp.int16)
    cell_x.start()
    first_bin.start()
    transform(1)
    sort_rows()
    for f in range(16):
        second_send[f] = spread_ref[f * 128 : (f + 1) * 128, :].reshape(8, 16, DEV).astype(BF16)
    second_freq.start()
    list_runs(carry, upper, row_i, list_ref, edge_ref)
    first_bin.wait_recv()
    first_freq.start()
    cell_x.wait_recv()
    cell_core.start()
    cell_core.wait_recv()
    for c in range(2):
        for x in range(4):
            at = (x * 2 + c) * DEV
            code_wide[at : at + DEV, :] = cell_all[c, x].astype(F32)
    stride = TR + 16
    for blk in range(8):
        code = code_wide[pl.ds(blk, DEV, stride=8), :].T.astype(I32)
        cell_rows_ref[blk * DEV : (blk + 1) * DEV, :] = (code >> 6).astype(F32)
        cell_rows_ref[stride + blk * DEV : stride + (blk + 1) * DEV, :] = (code & 63).astype(F32)
    for digit in range(2):
        cell_rows_ref[digit * stride + TR : (digit + 1) * stride, :] = jnp.zeros((16, DEV), F32)
    second_freq.wait_recv()
    second_bin.start()
    first_freq.wait_recv()
    second_bin.wait_recv()
    for part in (cell_freq, cell_x, cell_core, first_bin, first_freq, second_freq, second_bin):
        part.wait_send()


def layout_kernel(
    count_ref,
    start_ref,
    list_ref,
    edge_ref,
    first_ref,
    second_ref,
    cell_ref,
    dense_ref,
    first_wide,
    second_wide,
    rows_ref,
    raw_ref,
):
    stride = TR + 16
    for b in range(8):
        second_wide[b * 256 : (b + 1) * 256, :] = second_ref[b].reshape(256, DEV).astype(F32)
        for f in range(16):
            at = (b * 16 + f) * 16
            first_wide[at : at + 16, :] = first_ref[f, b].astype(F32)
    for blk in range(8):
        for part in range(2):
            pick = pl.ds(part * 8 + blk, DEV, stride=16)
            rows_ref[pl.ds(part * stride + blk * DEV, DEV), :] = first_wide[pick, :].T
            rows_ref[pl.ds((2 + part) * stride + blk * DEV, DEV), :] = second_wide[pick, :].T
    pad = jnp.zeros((16, DEV), F32)
    for comp in range(4):
        rows_ref[pl.ds(comp * stride + TR, 16), :] = pad

    sub32 = lax.broadcasted_iota(I32, (32, DEV), 0).astype(F32).astype(BF16)
    sub64 = lax.broadcasted_iota(I32, (64, DEV), 0).astype(F32).astype(BF16)
    one, zero = jnp.ones((), BF16), jnp.zeros((), BF16)

    def lay_out(run, size):
        count = count_ref[0, run]
        start = start_ref[0, run]
        left, right = [], []
        for j in range(size):
            at = start + j
            high = jnp.broadcast_to(cell_ref[pl.ds(at, 1), :], (16, DEV))
            high = jnp.where(j < count, high, -1.0).astype(BF16)
            hit = jnp.concatenate([high] * 2, axis=0) == sub32
            parts = []
            for comp in range(4):
                row = jnp.broadcast_to(rows_ref[pl.ds(comp * stride + at, 1), :], (16, DEV)).astype(BF16)
                parts.append(jnp.where(hit, jnp.concatenate([row] * 2, axis=0), zero))
            left.append(jnp.concatenate(parts, axis=0))
            low = jnp.broadcast_to(cell_ref[pl.ds(stride + at, 1), :], (16, DEV)).astype(BF16)
            right.append(jnp.where(jnp.concatenate([low] * 4, axis=0) == sub64, one, zero))
        raw_ref[run, :, 0:64] = lax.dot_general(
            jnp.concatenate(left, axis=1),
            jnp.concatenate(right, axis=1),
            (((1,), (1,)), ((), ())),
            preferred_element_type=F32,
        )

    begin = 0
    for kind, (size, together) in enumerate(((4, 32), (8, 32), (16, 16))):
        end = edge_ref[0, kind]

        def some_runs(step, _, begin=begin, end=end, size=size, together=together):
            for u in range(together):
                lay_out(list_ref[0, jnp.minimum(begin + step * together + u, end - 1)], size)
            return 0

        lax.fori_loop(0, (end - begin + together - 1) // together, some_runs, 0)
        begin = end

    top = lax.broadcasted_iota(I32, (8, DEV), 0) < 4
    left_half = lax.broadcasted_iota(I32, (8, DEV), 1) < 64

    def four_runs(group, _):
        for comp in range(4):
            at = pl.ds(pl.multiple_of(comp * ORDER + group * 16, 16), 16)
            for tile in range(4):
                sl = pl.ds(comp * 32 + 8 * tile, 8)
                merged = []
                for pair in range(2):
                    even = raw_ref[4 * group + 2 * pair, sl, :]
                    odd = raw_ref[4 * group + 2 * pair + 1, sl, :]
                    right = pltpu.roll(pltpu.roll(jnp.where(top, odd, even), 4, 0), 64, 1)
                    merged.append(jnp.where(left_half, jnp.where(top, even, odd), right))
                dense_ref[at, pl.ds(tile * DEV, DEV)] = jnp.concatenate(merged, axis=0).astype(BF16)
        return 0

    lax.fori_loop(0, DEV // 4, four_runs, 0, unroll=2)


def product_kernel(filt_ref, dense_ref, out_ref, hold_ref, block_ref, load_sem, send, recv):
    loads = []
    for i in range(2):
        part = pl.ds(2 * i * ORDER, 2 * ORDER)
        loads.append(pltpu.make_async_copy(dense_ref.at[part], hold_ref.at[part], load_sem.at[i]))
        loads[-1].start()
    mine = lax.axis_index("bin") * 2
    amplitude = 1.0 / math.sqrt(ORDER)
    greet((("bin", 8),))
    moves = [
        Exchange(
            "bin",
            8,
            lambda b, i=i: block_ref.at[b, i],
            lambda me, i=i: out_ref.at[:, me * 2 + i],
            send.at[i],
            recv.at[i],
            peers=far_first,
        )
        for i in range(2)
    ]
    for i in range(2):
        loads[i].wait()
        real = hold_ref[pl.ds(2 * i * ORDER, ORDER), :]
        imag = hold_ref[pl.ds((2 * i + 1) * ORDER, ORDER), :]
        fr = filt_ref[0, mine + i]
        fi = filt_ref[1, mine + i]
        for t in range(2):
            cols = slice(t * 256, (t + 1) * 256)
            rc, ic = real[:, cols], imag[:, cols]
            dot = functools.partial(jnp.dot, preferred_element_type=F32)
            sr = dot(real, rc) - dot(imag, ic)
            si = dot(real, ic) + dot(imag, rc)
            outr = ((fr * sr - fi * si) * amplitude).astype(BF16)
            outi = ((fr * si + fi * sr) * amplitude).astype(BF16)
            for b in range(8):
                block_ref[b, i, 0, :, cols] = outr[b * 64 : (b + 1) * 64]
                block_ref[b, i, 1, :, cols] = outi[b * 64 : (b + 1) * 64]
        if i == 0:
            pl.semaphore_wait(pltpu.get_barrier_semaphore(), 7)
        moves[i].start()
    for move in moves:
        move.wait_recv()
        move.wait_send()


def hand_over(rows_ref, out_ref, hold_ref, sem):
    loads = [pltpu.make_async_copy(rows_ref.at[:, i], hold_ref.at[:, i], sem.at[0, i]) for i in range(16)]
    stores = [pltpu.make_async_copy(hold_ref.at[:, i], out_ref.at[:, i], sem.at[1, i]) for i in range(16)]
    for load in loads:
        load.start()
    for load, store in zip(loads, stores):
        load.wait()
        store.start()
    for store in stores:
        store.wait()


def local(traces, rcv_index, src_index, wave_filter):
    tables = dft_tables()
    params = pltpu.CompilerParams(vmem_limit_bytes=LIMIT)
    vmem = pl.BlockSpec(memory_space=pltpu.VMEM)
    smem = pl.BlockSpec(memory_space=pltpu.SMEM)
    anywhere = pl.BlockSpec(memory_space=pl.ANY)
    shape = jax.ShapeDtypeStruct
    small = shape((8, DEV), I32)
    dma = pltpu.SemaphoreType.DMA
    outgoing, middle = pltpu.VMEM((8, 16, 16, DEV), BF16), pltpu.VMEM((16, 8, 16, DEV), BF16)
    first, second, cells, count, start, listed, edge = pl.pallas_call(
        spectrum_kernel,
        in_specs=[vmem, vmem, anywhere, anywhere, anywhere],
        out_specs=(anywhere, anywhere, vmem, vmem, vmem, vmem, vmem),
        out_shape=(
            shape((16, 8, 16, DEV), BF16),
            shape((8, 16, 16, DEV), BF16),
            shape((2 * (TR + 16), DEV), F32),
            small,
            small,
            small,
            small,
        ),
        scratch_shapes=[
            pltpu.VMEM((TR, NT), BF16),
            pltpu.VMEM((2, NT, 4 * DEV), BF16),
            pltpu.VMEM((TR, TR), BF16),
            pltpu.VMEM((TR, 256), BF16),
            pltpu.VMEM((2048, DEV), F32),
            pltpu.VMEM((8, DEV), I32),
            pltpu.VMEM((16, 8, DEV), I32),
            pltpu.VMEM((DEV, DEV), jnp.int16),
            pltpu.VMEM((2, 4, DEV, DEV), jnp.int16),
            pltpu.VMEM((TR, DEV), F32),
            outgoing,
            outgoing,
            middle,
            middle,
            dma((6,)),
            dma((3, 8)),
            dma((3, 8)),
            dma((3, 16)),
            dma((3, 16)),
            dma((2,)),
            dma((2,)),
        ],
        compiler_params=pltpu.CompilerParams(vmem_limit_bytes=LIMIT, collective_id=1, has_side_effects=True),
        cost_estimate=pl.CostEstimate(flops=5 * 10**9, bytes_accessed=9 * 10**6, transcendentals=0),
        name="spectrum",
    )(rcv_index.reshape(8, DEV), src_index.reshape(8, DEV), traces, jnp.asarray(tables[0]), jnp.asarray(tables[1]))
    dense = pl.pallas_call(
        layout_kernel,
        in_specs=[smem, smem, smem, smem, vmem, vmem, vmem],
        out_specs=vmem,
        out_shape=shape((4 * ORDER, ORDER), BF16),
        scratch_shapes=[
            pltpu.VMEM((2048, DEV), F32),
            pltpu.VMEM((2048, DEV), F32),
            pltpu.VMEM((4 * (TR + 16), DEV), F32),
            pltpu.VMEM((DEV, DEV, DEV), F32),
        ],
        compiler_params=params,
        name="layout",
    )(count, start, listed, edge, first, second, cells)
    rows = pl.pallas_call(
        product_kernel,
        in_specs=[smem, anywhere],
        out_specs=anywhere,
        out_shape=shape((2, 16, 64, ORDER), BF16),
        scratch_shapes=[
            pltpu.VMEM((4 * ORDER, ORDER), BF16),
            pltpu.VMEM((8, 2, 2, 64, ORDER), BF16),
            dma((2,)),
            dma((2, 8)),
            dma((2, 8)),
        ],
        compiler_params=pltpu.CompilerParams(vmem_limit_bytes=LIMIT, collective_id=2, has_side_effects=True),
        name="product",
    )(wave_filter, dense)
    return pl.pallas_call(
        hand_over,
        in_specs=[anywhere],
        out_specs=anywhere,
        out_shape=shape((2, 16, 64, ORDER), BF16),
        scratch_shapes=[pltpu.VMEM((2, 16, 64, ORDER), BF16), dma((2, 16))],
        compiler_params=params,
        name="hand_over",
    )(rows)


def solution(mesh):
    placed = (P(("bin", "freq"), None), P(("bin", "freq")), P(("bin", "freq")), P(None, "freq"))
    return jax.shard_map(
        local, mesh=mesh, in_specs=placed, out_specs=P(None, "freq", "bin", None), check_vma=False
    )
```
